1024 devices in a mesh: dp: 16 (over x, core), expert: 8 (over y), tensor: 8 (over z).
Axes of the slice: x: 8, y: 8, z: 8, core: 2. Of those that a mesh axis runs over, the one named last changes fastest.
Arguments:
- routes: int32 [8192, 2], P(('expert', 'tensor')), may hold values from 0 to 63, all different within a row; in each aligned block of 128 rows (0 to 127, 128 to 255, ...) at most 6 rows name the same one
- gate_scores: float32 [8192, 2], P(('expert', 'tensor')), may hold values from 0.1 to 1
- back_hidden: bfloat16 [64, 2432, 384], P(('expert', 'tensor'), 'dp'), may hold values from -6 to 6
- saved_gate: bfloat16 [64, 2432, 384], P(('expert', 'tensor'), 'dp'), may hold values from -6 to 6
- saved_up: bfloat16 [64, 2432, 384], P(('expert', 'tensor'), 'dp'), may hold values from -6 to 6
- expert_gate_w: bfloat16 [64, 2432, 3584], P(('expert', 'tensor'), 'dp'), may hold values from -0.09375 to 0.09375
- expert_up_w: bfloat16 [64, 2432, 3584], P(('expert', 'tensor'), 'dp'), may hold values from -0.09375 to 0.09375
- inputs_b: bfloat16 [3584, 32768], P('dp', ('expert', 'tensor')), may hold values from -6 to 6
- dense_gate_w: bfloat16 [2432, 3584], P('dp'), may hold values from -0.09375 to 0.09375
- dense_up_w: bfloat16 [2432, 3584], P('dp'), may hold values from -0.09375 to 0.09375
- dense_down_w: bfloat16 [2432, 3584], P('dp'), may hold values from -0.125 to 0.125
Outputs:
- grad_in_a: bfloat16 [3584, 8192], P('dp', ('expert', 'tensor'))
- dense_out_b: bfloat16 [3584, 32768], P('dp', ('expert', 'tensor'))
The draws below stay inside these ranges and needn't reach their ends.
Inputs may be any that keep to these rules, and one draw needn't show every extreme that they name: `routes`: the two experts of a token differ. Among the 128 tokens of one group no expert is named more than 6 times, a bound that some block reaches in every draw.
All inputs are finite; a program needn't handle non-finite values.
Results may differ from the reference program's by a relative error of at most 0.024.
Values may be sent and summed in bfloat16 or wider, within the bound.
A program may use at most 64 MiB of HBM per device.

```python
import math
import jax
import jax.numpy as jnp
import numpy as np
from jax import lax

D = 3584
FFE = 2432
FFD = 2432
TOK_A = 128
EXPERTS = 64
CAP = 6
SLOTS = 384
TOKENS_A = 8192
TOKENS_B = 32768
N_DP = 16


def shard_levels(stream_key, extent, cuts, smallest, high):
    level, own = 1.0, jax.random.fold_in(stream_key, 6)
    for axis_at, blocks in cuts:
        heights = jnp.exp(jax.random.uniform(jax.random.fold_in(own, axis_at), (blocks,), jnp.float32, smallest / len(cuts), high / len(cuts)))
        level = level * jnp.repeat(heights, extent[axis_at] // blocks).reshape([-1 if axis == axis_at else 1 for axis in range(len(extent))])
    return level


def deal_out(key, own, number, rows, amount, top, reach, lean):
    sequence = jax.random.permutation(key, amount)
    crowded, usual = load_shares(amount, rows * top, reach, lean, True), load_shares(amount, rows * top, reach, lean, False)
    places = jnp.arange(amount)

    def named(tallies, rotation):
        used = int((tallies > 0).sum())
        fixed = max(1, used // 4)
        moved = fixed + (places - fixed + rotation * (used - fixed)) % max(1, amount - fixed)
        return jnp.zeros((amount,), jnp.int32).at[sequence[jnp.where(places < fixed, places, moved)]].set(jnp.asarray(tallies, jnp.int32))

    tallies = jnp.where(number % 4 == 0, named(crowded, number // 4), named(usual, number - number // 4 - 1))
    mixed = jax.random.permutation(jax.random.fold_in(own, 3), amount)
    giver, taker = mixed[0:amount // 2 * 2:2], mixed[1:amount // 2 * 2:2]
    margin = jnp.minimum(tallies[giver] - 1, reach - tallies[taker]) // 2
    margin = jnp.where((giver == sequence[0]) | (taker == sequence[0]) | (tallies[taker] == 0), 0, jnp.maximum(margin, 0))
    moved = jax.random.randint(jax.random.fold_in(own, 4), (amount // 2,), 0, 1 << 20) % (margin + 1)
    tallies = tallies.at[giver].add(-moved).at[taker].add(moved)
    items = jnp.searchsorted(jnp.cumsum(tallies), jnp.arange(rows * top), side="right").astype(jnp.int32)
    table = items.reshape(top, rows).T
    table = table[jax.random.permutation(jax.random.fold_in(own, 1), rows)]
    rotation = jax.random.randint(jax.random.fold_in(own, 2), (rows, 1), 0, top)
    return jnp.take_along_axis(table, (jnp.arange(top)[None, :] + rotation) % top, axis=1)


def load_shares(amount, total, bound, lean, full):
    loads = [(1 << 20) // math.isqrt(standing ** lean) + 1 for standing in range(1, amount + 1)]
    largest = bound if full else min(bound, max(-(-total // amount), total * loads[0] // sum(loads)))
    least = 1 if total - largest >= amount - 1 else 0
    given, rest = [largest] + [least] * (amount - 1), total - largest - least * (amount - 1)
    while rest > 0:
        free = [i for i in range(1, amount) if given[i] < largest] or [i for i in range(1, amount) if given[i] < bound]
        mass, budget = sum([loads[i] for i in free]), rest
        for i in free:
            more = min(bound - given[i], max(1, budget * loads[i] // mass), rest)
            given[i] = given[i] + more
            rest = rest - more
    return np.array(given)


def noise(key, dims, scale, reach, cuts=(), kind=jnp.bfloat16):
    values = scale * jax.random.normal(key, dims, jnp.float32)
    if cuts:
        values = values * shard_levels(key, dims, cuts, -0.22, 0.18)
    return jnp.clip(values, -reach, reach).astype(kind)


def setup_inputs(seed: int = 0) -> dict:
    key_of = jax.random.split(jax.random.key(seed), 12)
    routes_keys = jax.random.split(jax.random.fold_in(key_of[0], 1), TOKENS_A // TOK_A)
    routes_turns = jax.random.permutation(jax.random.fold_in(key_of[0], 3), TOKENS_A // TOK_A)
    routes = jax.vmap(lambda own, number: deal_out(jax.random.fold_in(key_of[0], 2), own, number, TOK_A, EXPERTS, 2, CAP, 2))(routes_keys, routes_turns).reshape((TOKENS_A, 2))
    gate_scores = jnp.clip(0.1 + 0.9 * jax.random.uniform(key_of[1], (TOKENS_A, 2), jnp.float32) ** shard_levels(key_of[1], (TOKENS_A, 2), ((0, 64),), -0.2, 0.2), 0.1, 1.0)
    back_hidden = noise(key_of[2], (EXPERTS, FFE, SLOTS), 1.0, 6.0, ((0, 64), (1, 16)))
    saved_gate = noise(key_of[3], (EXPERTS, FFE, SLOTS), 1.5, 6.0, ((0, 64), (1, 16)))
    saved_up = noise(key_of[4], (EXPERTS, FFE, SLOTS), 1.0, 6.0, ((0, 64), (1, 16)))
    expert_gate_w = noise(key_of[5], (EXPERTS, FFE, D), D ** -0.5, 0.09375, ((0, 64), (1, 16)))
    expert_up_w = noise(key_of[6], (EXPERTS, FFE, D), D ** -0.5, 0.09375, ((0, 64), (1, 16)))
    inputs_b = noise(key_of[7], (D, TOKENS_B), 1.0, 6.0, ((0, 16), (1, 64)))
    dense_gate_w = noise(key_of[8], (FFD, D), D ** -0.5, 0.09375, ((0, 16),))
    dense_up_w = noise(key_of[9], (FFD, D), D ** -0.5, 0.09375, ((0, 16),))
    dense_down_w = noise(key_of[10], (FFD, D), FFD ** -0.5, 0.125, ((0, 16),))
    return dict(routes=routes, gate_scores=gate_scores, back_hidden=back_hidden, saved_gate=saved_gate, saved_up=saved_up, expert_gate_w=expert_gate_w, expert_up_w=expert_up_w, inputs_b=inputs_b, dense_gate_w=dense_gate_w, dense_up_w=dense_up_w, dense_down_w=dense_down_w)


def slot_table(routes):
    groups = routes.shape[0] // TOK_A
    flattened = routes.reshape(groups, TOK_A * 2)
    onehot = (flattened[:, :, None] == jnp.arange(EXPERTS, dtype=jnp.int32)[None, None, :]).astype(jnp.int32)
    before = jnp.cumsum(onehot, axis=1) - onehot
    position = jnp.sum(before * onehot, axis=2)
    column = jnp.arange(groups, dtype=jnp.int32)[:, None] * CAP + position
    return column.reshape(groups * TOK_A, 2).astype(jnp.int32)


def reference(routes, gate_scores, back_hidden, saved_gate, saved_up, expert_gate_w, expert_up_w, inputs_b, dense_gate_w, dense_up_w, dense_down_w):
    column = slot_table(routes)
    share_size = FFE // N_DP

    def one_expert(expert_items):
        back_b, gate_pre_b, up_pre_b, weight_gate, weight_up = expert_items
        back = back_b.astype(jnp.float32)
        gate_pre = gate_pre_b.astype(jnp.float32)
        up_pre = up_pre_b.astype(jnp.float32)
        sigmoid_g = jax.nn.sigmoid(gate_pre)
        grad_gate = (back * up_pre * sigmoid_g * (1.0 + gate_pre * (1.0 - sigmoid_g))).astype(jnp.bfloat16)
        grad_up = (back * gate_pre * sigmoid_g).astype(jnp.bfloat16)
        summed = jnp.zeros((D, SLOTS), jnp.float32)
        for member in range(N_DP):
            low = member * share_size
            share_term = jnp.dot(jnp.transpose(weight_gate[low:low + share_size]), grad_gate[low:low + share_size], preferred_element_type=jnp.float32)
            share_term = share_term + jnp.dot(jnp.transpose(weight_up[low:low + share_size]), grad_up[low:low + share_size], preferred_element_type=jnp.float32)
            rounded = lax.optimization_barrier(share_term.astype(jnp.bfloat16))
            summed = summed + rounded.astype(jnp.float32)
        return summed.astype(jnp.bfloat16)

    returned = lax.map(one_expert, (back_hidden, saved_gate, saved_up, expert_gate_w, expert_up_w))
    first_route = returned[routes[:, 0], :, column[:, 0]].astype(jnp.float32)
    second_route = returned[routes[:, 1], :, column[:, 1]].astype(jnp.float32)
    weighted = gate_scores[:, 0:1] * first_route + gate_scores[:, 1:2] * second_route
    grad_in_a = jnp.transpose(weighted).astype(jnp.bfloat16)

    dense_gate = jnp.dot(dense_gate_w, inputs_b, preferred_element_type=jnp.float32)
    dense_up = jnp.dot(dense_up_w, inputs_b, preferred_element_type=jnp.float32)
    dense_hidden = (jax.nn.silu(dense_gate) * dense_up).astype(jnp.bfloat16)
    dense_share = FFD // N_DP
    dense_sum = jnp.zeros((D, inputs_b.shape[1]), jnp.float32)
    for member in range(N_DP):
        low = member * dense_share
        share_term = jnp.dot(jnp.transpose(dense_down_w[low:low + dense_share]), dense_hidden[low:low + dense_share], preferred_element_type=jnp.float32)
        rounded = lax.optimization_barrier(share_term.astype(jnp.bfloat16))
        dense_sum = dense_sum + rounded.astype(jnp.float32)
    return grad_in_a, dense_sum.astype(jnp.bfloat16)
```

```python
import functools

import jax
import jax.numpy as jnp
from jax import lax
from jax.experimental import pallas as pl
from jax.experimental.pallas import tpu as pltpu
from jax.sharding import PartitionSpec as P

MESH = pl.DeviceIdType.MESH
BF = jnp.bfloat16
F32 = jnp.float32
TN = (((0,), (0,)), ((), ()))
NT = (((1,), (1,)), ((), ()))


def kernel(
    nx, ny, nz, cap,
    routes_h, scores_h, back_h, sgate_h, sup_h, egw_h, euw_h, inb_h, dgw_h, duw_h, ddw_h,
    grad_o, dense_o,
    routes_v, scores_v, back_v, sgate_v, sup_v, egw_v, euw_v, dgw_v, duw_v, ddw_v,
    x_all, pe, qe, pd, qd, se, re, sd, rd,
    gg_v, gu_v, hid_v, ef_v, a1, a2, a3, a4, whi, wlo, perm,
    load_sem, ag_s, ag_r, sib_s, sib_r, qe_s, qe_r, qd_s, qd_r, se_s, re_s, sd_s, rd_s, y_s, y_r, z_s, z_r,
):
    feat = inb_h.shape[0]
    half = feat // 2
    slots = back_h.shape[2]
    toks = inb_h.shape[1]
    pair = 4 * feat
    npair = nx // 2
    far = nx // 2
    me = lax.axis_index("dp")
    x, c = me // 2, me % 2
    y, z = lax.axis_index("expert"), lax.axis_index("tensor")
    sib = x * 2 + 1 - c

    def chip(offset):
        return (x + offset + nx) % nx

    def dp_of(offset):
        return chip(offset) * 2 + c

    def rdma(src, dst, ssem, rsem, **where):
        return pltpu.make_async_remote_copy(
            src_ref=src, dst_ref=dst, send_sem=ssem, recv_sem=rsem, device_id=where, device_id_type=MESH
        )

    def rows(start, size):
        return pl.ds(pl.multiple_of(start, 16), size)

    loads = []
    sources = (sgate_h.at[0], back_h.at[0], sup_h.at[0], egw_h.at[0], euw_h.at[0], routes_h, scores_h, dgw_h, duw_h, ddw_h)
    targets = (sgate_v, back_v, sup_v, egw_v, euw_v, routes_v, scores_v, dgw_v, duw_v, ddw_v)
    for i, (src, dst) in enumerate(zip(sources, targets)):
        loads.append(pltpu.make_async_copy(src, dst, load_sem.at[i]))
    own_x = pltpu.make_async_copy(inb_h, x_all.at[rows(me * feat, feat), :], load_sem.at[len(sources)])
    own_x.start()
    for load in loads:
        load.start()

    barrier = pltpu.get_barrier_semaphore()
    partners = [dict(dp=dp_of(1)), dict(dp=dp_of(-1)), dict(dp=sib)]
    partners += [dict(expert=(y + k) % ny) for k in range(1, ny)]
    partners += [dict(tensor=(z + k) % nz) for k in range(1, nz)]
    for partner in partners:
        pl.semaphore_signal(barrier, inc=1, device_id=partner, device_id_type=MESH)
    pl.semaphore_wait(barrier, len(partners))

    pending = []

    def go(copy):
        copy.start()
        pending.append(copy)

    def x_rows(dp, h):
        return x_all.at[rows(dp * feat + h * half, half), :]

    def ag_send(d, hop, h):
        sign = 1 - 2 * d
        origin = dp_of(-sign * (hop - 1))
        src = inb_h.at[pl.ds(h * half, half), :] if hop == 1 else x_rows(origin, h)
        go(rdma(src, x_rows(origin, h), ag_s.at[d, hop - 1, h], ag_r.at[d, hop - 1, h], dp=dp_of(sign)))

    def ag_recv(d, hop, h):
        sign = 1 - 2 * d
        origin = dp_of(-sign * hop)
        ref = x_rows(origin, h)
        rdma(ref, ref, ag_s.at[d, hop - 1, h], ag_r.at[d, hop - 1, h], dp=dp_of(sign)).wait_recv()
        return origin

    def sib_send(slot, src, origin, h):
        go(rdma(src, x_rows(origin, h), sib_s.at[slot], sib_r.at[slot], dp=sib))

    def sib_recv(slot, offset, h):
        ref = x_rows(chip(offset) * 2 + 1 - c, h)
        rdma(ref, ref, sib_s.at[slot], sib_r.at[slot], dp=sib).wait_recv()

    def ag_pieces(hop):
        pieces = [(d, h) for h in range(2) for d in range(2)]
        if hop == far:
            pieces = [(d, h) for d, h in pieces if d == h]
        return pieces

    def ag_step(hop):
        for d, h in ag_pieces(hop):
            origin = ag_recv(d, hop, h)
            if hop < far and (hop + 1 < far or d == h):
                ag_send(d, hop + 1, h)
            sib_send(2 + (hop - 1) * 4 + d * 2 + h, x_rows(origin, h), origin, h)

    for d, h in ag_pieces(1):
        ag_send(d, 1, h)
    for h in range(2):
        sib_send(h, inb_h.at[pl.ds(h * half, half), :], me, h)

    for i in range(3):
        loads[i].wait()
    gate_pre = sgate_v[...].astype(F32)
    back = back_v[...].astype(F32)
    sig = jax.nn.sigmoid(gate_pre)
    gg_v[...] = (back * sup_v[...].astype(F32) * sig * (1.0 + gate_pre * (1.0 - sig))).astype(BF)
    gu_v[...] = (back * gate_pre * sig).astype(BF)
    loads[3].wait()
    loads[4].wait()

    pair_order = [npair // 2] + [k for k in range(npair) if k not in (0, npair // 2)] + [0]

    def chip_pair(j):
        return (x // 2 + pair_order[j]) % npair

    def expert_pair(j):
        p = chip_pair(j)
        lanes = pl.ds(pl.multiple_of(p * pair, 128), pair)
        out = lax.dot_general(egw_v[:, lanes], gg_v[...], TN, preferred_element_type=F32)
        out = out + lax.dot_general(euw_v[:, lanes], gu_v[...], TN, preferred_element_type=F32)
        pe[rows(p * pair, pair), :] = out.astype(BF)
        for i in range(2):
            q_send(pe, qe, qe_s, qe_r, p * 2 + i, j * 2 + i)

    def q_rows(q, there):
        return q.at[rows(there * feat, feat), :]

    def q_send(p, q, ss, rs, there, slot):
        src = p.at[rows((there * 2 + 1 - c) * feat, feat), :]
        go(rdma(src, q_rows(q, there), ss.at[slot], rs.at[slot], dp=sib))

    def q_recv(q, ss, rs, j):
        for i in range(2):
            ref = q_rows(q, chip_pair(j) * 2 + i)
            rdma(ref, ref, ss.at[j * 2 + i], rs.at[j * 2 + i], dp=sib).wait_recv()

    def slot_of(hop, h):
        return 0 if hop == 0 else 1 + (hop - 1) * 2 + h

    def partial(p, q, there, h):
        own = p[rows((there * 2 + c) * feat + h * half, half), :].astype(F32)
        return own + q[rows(there * feat + h * half, half), :].astype(F32)

    def rs_copy(s, r, ss, rs, d, slot):
        return rdma(s.at[d, slot], r.at[d, slot], ss.at[d, slot], rs.at[d, slot], dp=dp_of(1 - 2 * d))

    def rs_send(flow, d, hop, h):
        p, q, s, r, ss, rs = flow
        slot = slot_of(hop, h)
        total = partial(p, q, chip((1 - 2 * d) * (far - hop)), h)
        if hop > 1 or (hop == 1 and h == d):
            before = slot_of(hop - 1, h)
            rs_copy(s, r, ss, rs, d, before).wait_recv()
            total = total + r[d, before].astype(F32)
        s[d, slot] = total.astype(BF)
        go(rs_copy(s, r, ss, rs, d, slot))

    def rs_open(flow):
        for d in range(2):
            rs_send(flow, d, 0, d)

    def rs_open_1(flow):
        for d in range(2):
            rs_send(flow, d, 1, 1 - d)

    def rs_step(flow, hop):
        for h in range(2):
            for d in range(2):
                if hop > 1 or h == d:
                    rs_send(flow, d, hop, h)

    def rs_final(flow, h):
        p, q, s, r, ss, rs = flow
        total = partial(p, q, x, h)
        for d in range(2):
            slot = slot_of(far - 1, h)
            rs_copy(s, r, ss, rs, d, slot).wait_recv()
            total = total + r[d, slot].astype(F32)
        return total.astype(BF)

    eflow = (pe, qe, se, re, se_s, re_s)
    dflow = (pd, qd, sd, rd, sd_s, rd_s)

    expert_pair(0)
    ag_step(1)
    expert_pair(1)
    expert_pair(2)
    ag_step(2)
    expert_pair(3)

    loads[5].wait()
    loads[6].wait()
    n_tok = routes_v.shape[0]
    lane = lax.broadcasted_iota(jnp.int32, (n_tok, n_tok), 1)
    row = lax.broadcasted_iota(jnp.int32, (n_tok, n_tok), 0)
    named = [routes_v[:, k:k + 1] for k in range(2)]
    hot = [jnp.where(lane == named[k], 1.0, 0.0).astype(F32) for k in range(2)]
    earlier = jnp.where(lane < row, 1.0, 0.0).astype(BF)
    count = jnp.dot(earlier, (hot[0] + hot[1]).astype(BF), preferred_element_type=F32)
    lane_s = lax.broadcasted_iota(jnp.int32, (n_tok, slots), 1).astype(F32)
    weighing = jnp.zeros((n_tok, slots), F32)
    for k in range(2):
        rank = jnp.sum(count * hot[k], axis=1, keepdims=True)
        place = ((named[k] % nz) * (ny * cap) + (named[k] // nz) * cap).astype(F32) + rank
        weighing = weighing + jnp.where(lane_s == place, scores_v[:, k:k + 1], 0.0)
    high = weighing.astype(BF)
    whi[...] = high
    wlo[...] = (weighing - high.astype(F32)).astype(BF)
    row_s = lax.broadcasted_iota(jnp.int32, (slots, slots), 0)
    lane_t = lax.broadcasted_iota(jnp.int32, (slots, slots), 1)
    i_s = lax.broadcasted_iota(jnp.int32, (slots, 1), 0)
    j_s = ((i_s % (ny * cap)) // cap) * (nz * cap) + (i_s // (ny * cap)) * cap + i_s % cap
    perm[...] = jnp.where(lane_t == j_s, 1.0, 0.0).astype(BF)

    ag_step(3)
    q_recv(qe, qe_s, qe_r, 0)
    rs_open(eflow)
    q_recv(qe, qe_s, qe_r, 1)
    q_recv(qe, qe_s, qe_r, 2)
    rs_open_1(eflow)
    ag_step(4)
    own_x.wait()
    for h in range(2):
        sib_recv(h, 0, h)
    for hop in range(1, far + 1):
        for d, h in ag_pieces(hop):
            sib_recv(2 + (hop - 1) * 4 + d * 2 + h, -(1 - 2 * d) * hop, h)

    for i in range(7, 10):
        loads[i].wait()
    rs_step(eflow, 1)
    gate = jnp.dot(dgw_v[...], x_all[...], preferred_element_type=F32)
    up = jnp.dot(duw_v[...], x_all[...], preferred_element_type=F32)
    hid_v[...] = (gate * jax.nn.sigmoid(gate) * up).astype(BF)
    rs_step(eflow, 2)

    def dense_pair(j):
        p = chip_pair(j)
        lanes = pl.ds(pl.multiple_of(p * pair, 128), pair)
        out = lax.dot_general(ddw_v[:, lanes], hid_v[...], TN, preferred_element_type=F32)
        pd[rows(p * pair, pair), :] = out.astype(BF)
        for i in range(2):
            q_send(pd, qd, qd_s, qd_r, p * 2 + i, j * 2 + i)

    dense_pair(0)
    dense_pair(1)
    q_recv(qd, qd_s, qd_r, 0)
    rs_open(dflow)
    dense_pair(2)
    q_recv(qe, qe_s, qe_r, 3)
    rs_step(eflow, 3)
    q_recv(qd, qd_s, qd_r, 1)
    q_recv(qd, qd_s, qd_r, 2)
    rs_open_1(dflow)
    dense_pair(3)
    rs_step(dflow, 1)

    ef_v[pl.ds(2 * half, ef_v.shape[0] - 2 * half), :] = jnp.zeros((ef_v.shape[0] - 2 * half, slots), BF)
    for h in range(2):
        ef_v[pl.ds(h * half, half), :] = rs_final(eflow, h)
    eye = jnp.where(lane_t == row_s, 1.0, 0.0).astype(BF)
    a1[...] = lax.dot_general(eye, ef_v[...], NT, preferred_element_type=F32).astype(BF)
    ny_rows, nz_rows = nz * cap, ny * cap

    def y_copy(k):
        return rdma(
            a1.at[rows((y + k) % ny * ny_rows, ny_rows), :], a2.at[rows(y * ny_rows, ny_rows), :],
            y_s.at[k], y_r.at[k], expert=(y + k) % ny,
        )

    def z_copy(k):
        return rdma(
            a3.at[rows((z + k) % nz * nz_rows, nz_rows), :], a4.at[rows(z * nz_rows, nz_rows), :],
            z_s.at[k], z_r.at[k], tensor=(z + k) % nz,
        )

    def y_wait(k):
        ref = a2.at[rows((y - k + ny) % ny * ny_rows, ny_rows), :]
        rdma(ref, ref, y_s.at[k], y_r.at[k], expert=(y + k) % ny).wait_recv()

    def z_wait(k):
        ref = a4.at[rows((z - k + nz) % nz * nz_rows, nz_rows), :]
        rdma(ref, ref, z_s.at[k], z_r.at[k], tensor=(z + k) % nz).wait_recv()

    for k in range(1, ny):
        go(y_copy(k))
    a2[rows(y * ny_rows, ny_rows), :] = a1[rows(y * ny_rows, ny_rows), :]
    rs_step(dflow, 2)
    for k in range(1, ny):
        y_wait(k)
    a3[...] = jnp.dot(perm[...], a2[...], preferred_element_type=F32).astype(BF)
    for k in range(1, nz):
        go(z_copy(k))
    a4[rows(z * nz_rows, nz_rows), :] = a3[rows(z * nz_rows, nz_rows), :]
    q_recv(qd, qd_s, qd_r, 3)
    rs_step(dflow, 3)
    for k in range(1, nz):
        z_wait(k)
    mixed = jnp.dot(whi[...], a4[...], preferred_element_type=F32)
    mixed = mixed + jnp.dot(wlo[...], a4[...], preferred_element_type=F32)
    grad_o[...] = mixed.T[:feat, :].astype(BF)
    for h in range(2):
        dense_o[pl.ds(h * half, half), :] = rs_final(dflow, h)
    for copy in pending:
        copy.wait_send()


def local(ny, nz, routes, gate_scores, back_hidden, saved_gate, saved_up, egw, euw, inputs_b, dgw, duw, ddw):
    feat, toks = inputs_b.shape
    hid, model = dgw.shape
    slots = back_hidden.shape[2]
    n_tok = routes.shape[0]
    nx = model // feat // 2
    far = nx // 2
    cap = slots // (ny * nz)
    half = feat // 2
    wide = -(-feat // 128) * 128
    steps = 2 * far - 1
    vm, dma = pltpu.VMEM, pltpu.SemaphoreType.DMA
    scratch = [
        vm((n_tok, 2), jnp.int32), vm((n_tok, 2), F32),
        vm((hid, slots), BF), vm((hid, slots), BF), vm((hid, slots), BF),
        vm((hid, model), BF), vm((hid, model), BF), vm((hid, model), BF), vm((hid, model), BF), vm((hid, model), BF),
        vm((model, toks), BF),
        vm((model, slots), BF), vm((model // 2, slots), BF), vm((model, toks), BF), vm((model // 2, toks), BF),
        vm((2, steps, half, slots), BF), vm((2, steps, half, slots), BF),
        vm((2, steps, half, toks), BF), vm((2, steps, half, toks), BF),
        vm((hid, slots), BF), vm((hid, slots), BF), vm((hid, toks), BF), vm((wide, slots), BF),
        vm((slots, wide), BF), vm((slots, wide), BF), vm((slots, wide), BF), vm((slots, wide), BF),
        vm((n_tok, slots), BF), vm((n_tok, slots), BF), vm((slots, slots), BF),
        dma((11,)),
        dma((2, far, 2)), dma((2, far, 2)), dma((2 + 4 * far,)), dma((2 + 4 * far,)),
        dma((nx,)), dma((nx,)), dma((nx,)), dma((nx,)),
        dma((2, steps)), dma((2, steps)), dma((2, steps)), dma((2, steps)),
        dma((ny,)), dma((ny,)), dma((nz,)), dma((nz,)),
    ]
    return pl.pallas_call(
        functools.partial(kernel, nx, ny, nz, cap),
        out_shape=(jax.ShapeDtypeStruct((feat, n_tok), BF), jax.ShapeDtypeStruct((feat, toks), BF)),
        in_specs=[pl.BlockSpec(memory_space=pl.ANY)] * 11,
        out_specs=(pl.BlockSpec(memory_space=pltpu.VMEM), pl.BlockSpec(memory_space=pltpu.VMEM)),
        scratch_shapes=scratch,
        compiler_params=pltpu.CompilerParams(
            collective_id=0, has_side_effects=True, vmem_limit_bytes=52 * 1024 * 1024
        ),
    )(routes, gate_scores, back_hidden, saved_gate, saved_up, egw, euw, inputs_b, dgw, duw, ddw)


def solution(mesh):
    both = ("expert", "tensor")
    in_specs = (
        P(both, None), P(both, None),
        P(both, "dp", None), P(both, "dp", None), P(both, "dp", None), P(both, "dp", None), P(both, "dp", None),
        P("dp", both), P("dp", None), P("dp", None), P("dp", None),
    )
    out_specs = (P("dp", both), P("dp", both))
    body = functools.partial(local, mesh.shape["expert"], mesh.shape["tensor"])
    return jax.shard_map(body, mesh=mesh, in_specs=in_specs, out_specs=out_specs, check_vma=False)
```

```python
import functools

import jax
import jax.numpy as jnp
from jax import lax
from jax.experimental import pallas as pl
from jax.experimental.pallas import tpu as pltpu
from jax.sharding import PartitionSpec as P

MESH = pl.DeviceIdType.MESH
BF = jnp.bfloat16
F32 = jnp.float32
TN = (((0,), (0,)), ((), ()))
NT = (((1,), (1,)), ((), ()))


def kernel(
    nx, ny, nz, cap,
    routes_h, scores_h, back_h, sgate_h, sup_h, egw_h, euw_h, inb_h, dgw_h, duw_h, ddw_h,
    grad_o, dense_o,
    routes_v, scores_v, back_v, sgate_v, sup_v, egw_v, euw_v, dgw_v, duw_v, ddw_v,
    x_all, pe, qe, pd, qd, se, re, sd, rd,
    gg_v, gu_v, ef_v, a1, a2, a3, a4, whi, wlo, perm,
    meet, load_sem, ag_s, ag_r, sib_s, sib_r, qe_s, qe_r, qd_s, qd_r, se_s, re_s, sd_s, rd_s, y_s, y_r, z_s, z_r,
):
    feat = inb_h.shape[0]
    half = feat // 2
    slots = back_h.shape[2]
    part = inb_h.shape[1] // 2
    pair = 4 * feat
    npair = nx // 2
    far = nx // 2
    me = lax.axis_index("dp")
    x, c = me // 2, me % 2
    y, z = lax.axis_index("expert"), lax.axis_index("tensor")
    sib = x * 2 + 1 - c

    def chip(offset):
        return (x + offset + nx) % nx

    def dp_of(offset):
        return chip(offset) * 2 + c

    def rdma(src, dst, ssem, rsem, **where):
        return pltpu.make_async_remote_copy(
            src_ref=src, dst_ref=dst, send_sem=ssem, recv_sem=rsem, device_id=where, device_id_type=MESH
        )

    def rows(start, size):
        return pl.ds(pl.multiple_of(start, 16), size)

    loads = []
    sources = (sgate_h.at[0], back_h.at[0], sup_h.at[0], egw_h.at[0], euw_h.at[0], routes_h, scores_h, dgw_h, duw_h, ddw_h)
    targets = (sgate_v, back_v, sup_v, egw_v, euw_v, routes_v, scores_v, dgw_v, duw_v, ddw_v)
    for i, (src, dst) in enumerate(zip(sources, targets)):
        loads.append(pltpu.make_async_copy(src, dst, load_sem.at[i]))
    own_x = pltpu.make_async_copy(inb_h, x_all.at[rows(me * feat, feat), :], load_sem.at[len(sources)])
    own_x.start()
    for load in loads:
        load.start()

    barrier = pltpu.get_barrier_semaphore()
    y_z = [dict(expert=(y + k) % ny) for k in range(1, ny)]
    y_z += [dict(tensor=(z + k) % nz) for k in range(1, nz)]

    def signal(sem, **where):
        pl.semaphore_signal(sem, inc=1, device_id=where, device_id_type=MESH)

    @pl.when(c == 0)
    def _():
        signal(barrier, dp=dp_of(1))
        signal(barrier, dp=dp_of(-1))
        pl.semaphore_wait(barrier, 3)
        signal(meet.at[0], dp=dp_of(1))
        signal(meet.at[0], dp=dp_of(-1))
        pl.semaphore_wait(meet.at[0], 2)
        signal(meet.at[1], dp=sib)

    @pl.when(c == 1)
    def _():
        signal(barrier, dp=sib)
        pl.semaphore_wait(meet.at[1], 1)
        for where in y_z:
            signal(barrier, **where)

    def meet_y_z():
        @pl.when(c == 1)
        def _():
            if y_z:
                pl.semaphore_wait(barrier, len(y_z))
            signal(meet.at[2], dp=sib)

        @pl.when(c == 0)
        def _():
            pl.semaphore_wait(meet.at[2], 1)

    pending = []

    def go(copy):
        copy.start()
        pending.append(copy)

    def x_part(dp, t, h, size):
        return x_all.at[rows(dp * feat + h * half, size), pl.ds(t * part, part)]

    def ag_copy(d, t, hop, h, origin):
        src = dst = x_part(origin, t, h, half)
        if hop == 1:
            src = inb_h.at[pl.ds(h * half, half), pl.ds(t * part, part)]
        return rdma(src, dst, ag_s.at[t, d, hop - 1, h], ag_r.at[t, d, hop - 1, h], dp=dp_of(1 - 2 * d))

    def sib_copy(t, slot, h, origin, size):
        src = dst = x_part(origin, t, h, size)
        if slot == 0:
            src = inb_h.at[:, pl.ds(t * part, part)]
        return rdma(src, dst, sib_s.at[t, slot], sib_r.at[t, slot], dp=sib)

    def ag_open(t):
        for h in range(2):
            for d in range(2):
                go(ag_copy(d, t, 1, h, me))
        go(sib_copy(t, 0, 0, me, feat))

    def ag_step(t, hop):
        for h in range(2):
            for d in range(2):
                if hop == far and h != d:
                    continue
                origin = dp_of(-(1 - 2 * d) * hop)
                ag_copy(d, t, hop, h, origin).wait_recv()
                if hop + 1 < far or (hop + 1 == far and h == d):
                    go(ag_copy(d, t, hop + 1, h, origin))
                go(sib_copy(t, 1 + (hop - 1) * 4 + d * 2 + h, h, origin, half))

    def sib_wait(t):
        sib_copy(t, 0, 0, sib, feat).wait_recv()
        for hop in range(1, far + 1):
            for h in range(2):
                for d in range(2):
                    if hop < far or h == d:
                        origin = chip(-(1 - 2 * d) * hop) * 2 + 1 - c
                        sib_copy(t, 1 + (hop - 1) * 4 + d * 2 + h, h, origin, half).wait_recv()

    for t in range(2):
        ag_open(t)

    for i in range(3):
        loads[i].wait()
    gate_pre = sgate_v[...].astype(F32)
    back = back_v[...].astype(F32)
    sig = jax.nn.sigmoid(gate_pre)
    gg_v[...] = (back * sup_v[...].astype(F32) * sig * (1.0 + gate_pre * (1.0 - sig))).astype(BF)
    gu_v[...] = (back * gate_pre * sig).astype(BF)
    loads[3].wait()
    loads[4].wait()

    pair_order = [npair // 2] + [k for k in range(npair) if k not in (0, npair // 2)] + [0]

    def chip_pair(j):
        return (x // 2 + pair_order[j]) % npair

    def expert_pair(j):
        p = chip_pair(j)
        lanes = pl.ds(pl.multiple_of(p * pair, 128), pair)
        out = lax.dot_general(egw_v[:, lanes], gg_v[...], TN, preferred_element_type=F32)
        out = out + lax.dot_general(euw_v[:, lanes], gu_v[...], TN, preferred_element_type=F32)
        pe[rows(p * pair, pair), :] = out.astype(BF)
        for i in range(2):
            q_send(pe, qe, qe_s, qe_r, p * 2 + i, j * 2 + i)

    def q_rows(q, there):
        return q.at[rows(there * feat, feat), :]

    def q_send(p, q, ss, rs, there, slot):
        src = p.at[rows((there * 2 + 1 - c) * feat, feat), :]
        go(rdma(src, q_rows(q, there), ss.at[slot], rs.at[slot], dp=sib))

    def q_recv(q, ss, rs, j):
        for i in range(2):
            ref = q_rows(q, chip_pair(j) * 2 + i)
            rdma(ref, ref, ss.at[j * 2 + i], rs.at[j * 2 + i], dp=sib).wait_recv()

    def slot_of(hop, h):
        return 0 if hop == 0 else 1 + (hop - 1) * 2 + h

    def partial(p, q, there, h):
        own = p[rows((there * 2 + c) * feat + h * half, half), :].astype(F32)
        return own + q[rows(there * feat + h * half, half), :].astype(F32)

    def rs_copy(s, r, ss, rs, d, slot):
        return rdma(s.at[d, slot], r.at[d, slot], ss.at[d, slot], rs.at[d, slot], dp=dp_of(1 - 2 * d))

    def rs_send(flow, d, hop, h):
        p, q, s, r, ss, rs = flow
        slot = slot_of(hop, h)
        total = partial(p, q, chip((1 - 2 * d) * (far - hop)), h)
        if hop > 1 or (hop == 1 and h == d):
            before = slot_of(hop - 1, h)
            rs_copy(s, r, ss, rs, d, before).wait_recv()
            total = total + r[d, before].astype(F32)
        s[d, slot] = total.astype(BF)
        go(rs_copy(s, r, ss, rs, d, slot))

    def rs_open(flow):
        for d in range(2):
            rs_send(flow, d, 0, d)

    def rs_open_1(flow):
        for d in range(2):
            rs_send(flow, d, 1, 1 - d)

    def rs_step(flow, hop, other):
        for d in range(2):
            rs_send(flow, d, hop, 1 - d if other else d)

    def rs_final(flow, h):
        p, q, s, r, ss, rs = flow
        total = partial(p, q, x, h)
        for d in range(2):
            slot = slot_of(far - 1, h)
            rs_copy(s, r, ss, rs, d, slot).wait_recv()
            total = total + r[d, slot].astype(F32)
        return total.astype(BF)

    eflow = (pe, qe, se, re, se_s, re_s)
    dflow = [tuple(ref.at[t] for ref in (pd, qd, sd, rd, sd_s, rd_s)) for t in range(2)]

    for j in range(npair):
        expert_pair(j)
    for t in range(2):
        ag_step(t, 1)
    q_recv(qe, qe_s, qe_r, 0)
    rs_open(eflow)
    for j in range(1, npair):
        q_recv(qe, qe_s, qe_r, j)
    rs_open_1(eflow)

    loads[5].wait()
    loads[6].wait()
    n_tok = routes_v.shape[1]
    lane = lax.broadcasted_iota(jnp.int32, (n_tok, n_tok), 1)
    row = lax.broadcasted_iota(jnp.int32, (n_tok, n_tok), 0)
    named = [routes_v[k:k + 1, :] for k in range(2)]
    hot = [jnp.where(row == named[k], 1.0, 0.0).astype(F32) for k in range(2)]
    earlier = jnp.where(row < lane, 1.0, 0.0).astype(BF)
    count = jnp.dot((hot[0] + hot[1]).astype(BF), earlier, preferred_element_type=F32)
    place_s = lax.broadcasted_iota(jnp.int32, (slots, n_tok), 0).astype(F32)
    weighing = jnp.zeros((slots, n_tok), F32)
    for k in range(2):
        rank = jnp.sum(count * hot[k], axis=0, keepdims=True)
        place = ((named[k] % nz) * (ny * cap) + (named[k] // nz) * cap).astype(F32) + rank
        weighing = weighing + jnp.where(place_s == place, scores_v[k:k + 1, :], 0.0)
    high = weighing.astype(BF)
    whi[...] = high
    wlo[...] = (weighing - high.astype(F32)).astype(BF)
    row_s = lax.broadcasted_iota(jnp.int32, (slots, slots), 0)
    lane_t = lax.broadcasted_iota(jnp.int32, (slots, slots), 1)
    i_s = lax.broadcasted_iota(jnp.int32, (slots, 1), 0)
    j_s = ((i_s % (ny * cap)) // cap) * (nz * cap) + (i_s // (ny * cap)) * cap + i_s % cap
    perm[...] = jnp.where(lane_t == j_s, 1.0, 0.0).astype(BF)

    for t in range(2):
        ag_step(t, 2)
    for t in range(2):
        ag_step(t, 3)
    rs_step(eflow, 1, False)
    ag_step(0, 4)
    rs_step(eflow, 2, True)

    def dense_part(t):
        sib_wait(t)
        block = x_all[:, t * part:(t + 1) * part]
        gate = jnp.dot(dgw_v[...], block, preferred_element_type=F32)
        up = jnp.dot(duw_v[...], block, preferred_element_type=F32)
        hidden = (gate * jax.nn.sigmoid(gate) * up).astype(BF)
        p_t, q_t, ss, rs = pd.at[t], qd.at[t], qd_s.at[t], qd_r.at[t]
        for j in range(npair):
            p = chip_pair(j)
            lanes = pl.ds(pl.multiple_of(p * pair, 128), pair)
            out = lax.dot_general(ddw_v[:, lanes], hidden, TN, preferred_element_type=F32)
            p_t[rows(p * pair, pair), :] = out.astype(BF)
            for i in range(2):
                q_send(p_t, q_t, ss, rs, p * 2 + i, j * 2 + i)

    def dense_recv(t, j):
        q_recv(qd.at[t], qd_s.at[t], qd_r.at[t], j)

    own_x.wait()
    for i in range(7, 10):
        loads[i].wait()
    dense_part(0)
    ag_step(1, 4)
    rs_step(eflow, 2, False)
    dense_recv(0, 0)
    rs_open(dflow[0])
    dense_recv(0, 1)
    dense_recv(0, 2)
    rs_open_1(dflow[0])
    rs_step(eflow, 3, True)
    dense_part(1)
    rs_step(eflow, 3, False)
    dense_recv(1, 0)
    rs_open(dflow[1])
    dense_recv(1, 1)
    dense_recv(1, 2)
    rs_open_1(dflow[1])
    rs_step(dflow[0], 1, False)

    ef_v[pl.ds(2 * half, ef_v.shape[0] - 2 * half), :] = jnp.zeros((ef_v.shape[0] - 2 * half, slots), BF)
    for h in range(2):
        ef_v[pl.ds(h * half, half), :] = rs_final(eflow, h)
    eye = jnp.where(lane_t == row_s, 1.0, 0.0).astype(BF)
    a1[...] = lax.dot_general(eye, ef_v[...], NT, preferred_element_type=F32).astype(BF)
    ny_rows, nz_rows = nz * cap, ny * cap

    def y_copy(k):
        return rdma(
            a1.at[rows((y + k) % ny * ny_rows, ny_rows), :], a2.at[rows(y * ny_rows, ny_rows), :],
            y_s.at[k], y_r.at[k], expert=(y + k) % ny,
        )

    def z_copy(k):
        return rdma(
            a3.at[rows((z + k) % nz * nz_rows, nz_rows), :], a4.at[rows(z * nz_rows, nz_rows), :],
            z_s.at[k], z_r.at[k], tensor=(z + k) % nz,
        )

    def y_wait(k):
        ref = a2.at[rows((y - k + ny) % ny * ny_rows, ny_rows), :]
        rdma(ref, ref, y_s.at[k], y_r.at[k], expert=(y + k) % ny).wait_recv()

    def z_wait(k):
        ref = a4.at[rows((z - k + nz) % nz * nz_rows, nz_rows), :]
        rdma(ref, ref, z_s.at[k], z_r.at[k], tensor=(z + k) % nz).wait_recv()

    meet_y_z()
    for k in range(1, ny):
        go(y_copy(k))
    a2[rows(y * ny_rows, ny_rows), :] = a1[rows(y * ny_rows, ny_rows), :]
    rs_step(dflow[1], 1, False)
    rs_step(dflow[0], 2, True)
    rs_step(dflow[0], 2, False)
    for k in range(1, ny):
        y_wait(k)
    a3[...] = jnp.dot(perm[...], a2[...], preferred_element_type=F32).astype(BF)
    for k in range(1, nz):
        go(z_copy(k))
    a4[rows(z * nz_rows, nz_rows), :] = a3[rows(z * nz_rows, nz_rows), :]
    rs_step(dflow[1], 2, True)
    rs_step(dflow[1], 2, False)
    dense_recv(0, 3)
    dense_recv(1, 3)
    rs_step(dflow[0], 3, True)
    rs_step(dflow[0], 3, False)
    rs_step(dflow[1], 3, True)
    rs_step(dflow[1], 3, False)
    for t in range(2):
        for h in range(2):
            dense_o[pl.ds(h * half, half), pl.ds(t * part, part)] = rs_final(dflow[t], h)
    for k in range(1, nz):
        z_wait(k)
    mixed = lax.dot_general(a4[...], whi[...], TN, preferred_element_type=F32)
    mixed = mixed + lax.dot_general(a4[...], wlo[...], TN, preferred_element_type=F32)
    grad_o[...] = mixed[:feat, :].astype(BF)
    for copy in pending:
        copy.wait_send()


def local(ny, nz, routes, gate_scores, back_hidden, saved_gate, saved_up, egw, euw, inputs_b, dgw, duw, ddw):
    feat, toks = inputs_b.shape
    hid, model = dgw.shape
    slots = back_hidden.shape[2]
    n_tok = routes.shape[0]
    nx = model // feat // 2
    far = nx // 2
    cap = slots // (ny * nz)
    half = feat // 2
    part = toks // 2
    wide = -(-feat // 128) * 128
    steps = 2 * far - 1
    vm, dma = pltpu.VMEM, pltpu.SemaphoreType.DMA
    scratch = [
        vm((2, n_tok), jnp.int32), vm((2, n_tok), F32),
        vm((hid, slots), BF), vm((hid, slots), BF), vm((hid, slots), BF),
        vm((hid, model), BF), vm((hid, model), BF), vm((hid, model), BF), vm((hid, model), BF), vm((hid, model), BF),
        vm((model, toks), BF),
        vm((model, slots), BF), vm((model // 2, slots), BF), vm((2, model, part), BF), vm((2, model // 2, part), BF),
        vm((2, steps, half, slots), BF), vm((2, steps, half, slots), BF),
        vm((2, 2, steps, half, part), BF), vm((2, 2, steps, half, part), BF),
        vm((hid, slots), BF), vm((hid, slots), BF), vm((wide, slots), BF),
        vm((slots, wide), BF), vm((slots, wide), BF), vm((slots, wide), BF), vm((slots, wide), BF),
        vm((slots, n_tok), BF), vm((slots, n_tok), BF), vm((slots, slots), BF),
        pltpu.SemaphoreType.REGULAR((3,)), dma((11,)),
        dma((2, 2, far, 2)), dma((2, 2, far, 2)), dma((2, 1 + 4 * far)), dma((2, 1 + 4 * far)),
        dma((nx,)), dma((nx,)), dma((2, nx)), dma((2, nx)),
        dma((2, steps)), dma((2, steps)), dma((2, 2, steps)), dma((2, 2, steps)),
        dma((ny,)), dma((ny,)), dma((nz,)), dma((nz,)),
    ]
    return pl.pallas_call(
        functools.partial(kernel, nx, ny, nz, cap),
        out_shape=(pltpu.VMEM((feat, n_tok), BF), pltpu.VMEM((feat, toks), BF)),
        in_specs=[pl.BlockSpec(memory_space=pltpu.HBM)] * 11,
        out_specs=(pl.BlockSpec(memory_space=pltpu.VMEM), pl.BlockSpec(memory_space=pltpu.VMEM)),
        scratch_shapes=scratch,
        compiler_params=pltpu.CompilerParams(
            collective_id=0, has_side_effects=True, vmem_limit_bytes=62 * 1024 * 1024
        ),
    )(routes.T, gate_scores.T, back_hidden, saved_gate, saved_up, egw, euw, inputs_b, dgw, duw, ddw)


def solution(mesh):
    both = ("expert", "tensor")
    in_specs = (
        P(both, None), P(both, None),
        P(both, "dp", None), P(both, "dp", None), P(both, "dp", None), P(both, "dp", None), P(both, "dp", None),
        P("dp", both), P("dp", None), P("dp", None), P("dp", None),
    )
    out_specs = (P("dp", both), P("dp", both))
    body = functools.partial(local, mesh.shape["expert"], mesh.shape["tensor"])
    return jax.shard_map(body, mesh=mesh, in_specs=in_specs, out_specs=out_specs, check_vma=False)
```

```python
import functools

import jax
import jax.numpy as jnp
from jax import lax
from jax.experimental import pallas as pl
from jax.experimental.pallas import tpu as pltpu
from jax.sharding import PartitionSpec as P

MESH = pl.DeviceIdType.MESH
BF = jnp.bfloat16
F32 = jnp.float32
TN = (((0,), (0,)), ((), ()))
NT = (((1,), (1,)), ((), ()))


def kernel(
    nx, ny, nz, cap,
    routes_h, scores_h, back_h, sgate_h, sup_h, egw_h, euw_h, inb_h, dgw_h, duw_h, ddw_h,
    grad_o, dense_o,
    routes_v, scores_v, back_v, sgate_v, sup_v, egw_v, euw_v, dgw_v, duw_v, ddw_v,
    x_all, h_all, w_all, w_cut, pe, qe, se, re,
    gg_v, gu_v, ef_v, a1, a2, a3, a4, whi, wlo, perm,
    meet, load_sem, ag_s, ag_r, sib_s, sib_r, hg_s, hg_r, hsib_s, hsib_r, wx_s, wx_r, wz_s, wz_r, wy_s, wy_r,
    qe_s, qe_r, se_s, re_s, y_s, y_r, z_s, z_r,
):
    feat = inb_h.shape[0]
    half = feat // 2
    hid_rows = h_all.shape[0] // (2 * nx)
    slots = back_h.shape[2]
    part = inb_h.shape[1] // 2
    pair = 4 * feat
    npair = nx // 2
    far = nx // 2
    me = lax.axis_index("dp")
    x, c = me // 2, me % 2
    y, z = lax.axis_index("expert"), lax.axis_index("tensor")
    sib = x * 2 + 1 - c

    def chip(offset):
        return (x + offset + nx) % nx

    def dp_of(offset):
        return chip(offset) * 2 + c

    def rdma(src, dst, ssem, rsem, **where):
        return pltpu.make_async_remote_copy(
            src_ref=src, dst_ref=dst, send_sem=ssem, recv_sem=rsem, device_id=where, device_id_type=MESH
        )

    def rows(start, size):
        return pl.ds(pl.multiple_of(start, 16), size)

    loads = []
    sources = (sgate_h.at[0], back_h.at[0], sup_h.at[0], egw_h.at[0], euw_h.at[0], routes_h, scores_h, dgw_h, duw_h, ddw_h)
    targets = (sgate_v, back_v, sup_v, egw_v, euw_v, routes_v, scores_v, dgw_v, duw_v, ddw_v)
    for i, (src, dst) in enumerate(zip(sources, targets)):
        loads.append(pltpu.make_async_copy(src, dst, load_sem.at[i]))
    own_x = pltpu.make_async_copy(inb_h, x_all.at[rows(me * feat, feat), :], load_sem.at[len(sources)])
    own_x.start()
    for load in loads:
        load.start()

    def gather(buf, size, own, ss, rs, sib_ss, sib_rs):
        part_rows = size // 2

        def piece(dp, t, h, n):
            return buf.at[rows(dp * size + h * part_rows, n), pl.ds(t * part, part)]

        def ring_copy(d, t, hop, h, origin):
            src = dst = piece(origin, t, h, part_rows)
            if hop == 1 and own is not None:
                src = own.at[pl.ds(h * part_rows, part_rows), pl.ds(t * part, part)]
            return rdma(src, dst, ss.at[t, d, hop - 1, h], rs.at[t, d, hop - 1, h], dp=dp_of(1 - 2 * d))

        def sib_copy(t, slot, h, origin, n):
            src = dst = piece(origin, t, h, n)
            if slot == 0 and own is not None:
                src = own.at[:, pl.ds(t * part, part)]
            return rdma(src, dst, sib_ss.at[t, slot], sib_rs.at[t, slot], dp=sib)

        def first(t):
            return [ring_copy(d, t, 1, h, me) for h in range(2) for d in range(2)] + [sib_copy(t, 0, 0, me, size)]

        def step(t, hop):
            for h in range(2):
                for d in range(2):
                    if hop == far and h != d:
                        continue
                    origin = dp_of(-(1 - 2 * d) * hop)
                    ring_copy(d, t, hop, h, origin).wait_recv()
                    if hop + 1 < far or (hop + 1 == far and h == d):
                        go(ring_copy(d, t, hop + 1, h, origin))
                    go(sib_copy(t, 1 + (hop - 1) * 4 + d * 2 + h, h, origin, part_rows))

        def finish(t):
            sib_copy(t, 0, 0, sib, size).wait_recv()
            for hop in range(1, far + 1):
                for h in range(2):
                    for d in range(2):
                        if hop < far or h == d:
                            origin = chip(-(1 - 2 * d) * hop) * 2 + 1 - c
                            sib_copy(t, 1 + (hop - 1) * 4 + d * 2 + h, h, origin, part_rows).wait_recv()

        return first, step, finish

    x_first, x_step, x_finish = gather(x_all, feat, inb_h, ag_s, ag_r, sib_s, sib_r)
    h_first, h_step, h_finish = gather(h_all, hid_rows, None, hg_s, hg_r, hsib_s, hsib_r)

    def x_copies():
        return x_first(0) + x_first(1)

    barrier = pltpu.get_barrier_semaphore()
    y_z = [dict(expert=(y + k) % ny) for k in range(1, ny)]
    y_z += [dict(tensor=(z + k) % nz) for k in range(1, nz)]

    def signal(sem, **where):
        pl.semaphore_signal(sem, inc=1, device_id=where, device_id_type=MESH)

    @pl.when(c == 0)
    def _():
        for k in range(1, nx):
            signal(barrier, dp=dp_of(k))
        pl.semaphore_wait(barrier, nx)
        for k in range(1, nx):
            signal(meet.at[0], dp=dp_of(k))
        for copy in x_copies():
            copy.start()
        pl.semaphore_wait(meet.at[0], nx - 1)
        signal(meet.at[1], dp=sib)

    @pl.when(c == 1)
    def _():
        signal(barrier, dp=sib)
        pl.semaphore_wait(meet.at[1], 1)
        for copy in x_copies():
            copy.start()
        for where in y_z:
            signal(barrier, **where)

    def meet_y_z():
        @pl.when(c == 1)
        def _():
            if y_z:
                pl.semaphore_wait(barrier, len(y_z))
            signal(meet.at[2], dp=sib)

        @pl.when(c == 0)
        def _():
            pl.semaphore_wait(meet.at[2], 1)

    pending = []

    def go(copy):
        copy.start()
        pending.append(copy)

    pending.extend(x_copies())

    for i in range(3):
        loads[i].wait()
    gate_pre = sgate_v[...].astype(F32)
    back = back_v[...].astype(F32)
    sig = jax.nn.sigmoid(gate_pre)
    gg_v[...] = (back * sup_v[...].astype(F32) * sig * (1.0 + gate_pre * (1.0 - sig))).astype(BF)
    gu_v[...] = (back * gate_pre * sig).astype(BF)
    loads[3].wait()
    loads[4].wait()

    pair_order = [npair // 2] + [k for k in range(npair) if k not in (0, npair // 2)] + [0]

    def chip_pair(j):
        return (x // 2 + pair_order[j]) % npair

    def expert_pair(j):
        p = chip_pair(j)
        lanes = pl.ds(pl.multiple_of(p * pair, 128), pair)
        out = lax.dot_general(egw_v[:, lanes], gg_v[...], TN, preferred_element_type=F32)
        out = out + lax.dot_general(euw_v[:, lanes], gu_v[...], TN, preferred_element_type=F32)
        pe[rows(p * pair, pair), :] = out.astype(BF)
        for i in range(2):
            q_send(pe, qe, qe_s, qe_r, p * 2 + i, j * 2 + i)

    def q_rows(q, there):
        return q.at[rows(there * feat, feat), :]

    def q_send(p, q, ss, rs, there, slot):
        src = p.at[rows((there * 2 + 1 - c) * feat, feat), :]
        go(rdma(src, q_rows(q, there), ss.at[slot], rs.at[slot], dp=sib))

    def q_recv(q, ss, rs, j):
        for i in range(2):
            ref = q_rows(q, chip_pair(j) * 2 + i)
            rdma(ref, ref, ss.at[j * 2 + i], rs.at[j * 2 + i], dp=sib).wait_recv()

    def slot_of(hop, h):
        return 0 if hop == 0 else 1 + (hop - 1) * 2 + h

    def partial(p, q, there, h):
        own = p[rows((there * 2 + c) * feat + h * half, half), :].astype(F32)
        return own + q[rows(there * feat + h * half, half), :].astype(F32)

    def rs_copy(s, r, ss, rs, d, slot):
        return rdma(s.at[d, slot], r.at[d, slot], ss.at[d, slot], rs.at[d, slot], dp=dp_of(1 - 2 * d))

    def rs_send(flow, d, hop, h):
        p, q, s, r, ss, rs = flow
        slot = slot_of(hop, h)
        total = partial(p, q, chip((1 - 2 * d) * (far - hop)), h)
        if hop > 1 or (hop == 1 and h == d):
            before = slot_of(hop - 1, h)
            rs_copy(s, r, ss, rs, d, before).wait_recv()
            total = total + r[d, before].astype(F32)
        s[d, slot] = total.astype(BF)
        go(rs_copy(s, r, ss, rs, d, slot))

    def rs_open(flow):
        for d in range(2):
            rs_send(flow, d, 0, d)

    def rs_open_1(flow):
        for d in range(2):
            rs_send(flow, d, 1, 1 - d)

    def rs_step(flow, hop, other):
        for d in range(2):
            rs_send(flow, d, hop, 1 - d if other else d)

    def rs_final(flow, h):
        p, q, s, r, ss, rs = flow
        total = partial(p, q, x, h)
        for d in range(2):
            slot = slot_of(far - 1, h)
            rs_copy(s, r, ss, rs, d, slot).wait_recv()
            total = total + r[d, slot].astype(F32)
        return total.astype(BF)

    eflow = (pe, qe, se, re, se_s, re_s)

    w_src = 2 * y + z // (nz // 2 or 1)
    w_half = hid_rows // 2

    def w_place(zz):
        return zz // 2 % 2 * w_half, pl.ds(pl.multiple_of(zz % 2 * 128, 128), 128)

    def w_part(zz):
        low, lanes = w_place(zz)
        return w_all.at[rows((2 * y + zz // (nz // 2 or 1)) * hid_rows + low, w_half), lanes]

    def w_x_copy(k):
        low, lanes = w_place(z)
        there = (me + k) % (2 * nx)
        return rdma(w_cut.at[there, rows(low, w_half), lanes], w_part(z), wx_s.at[k], wx_r.at[0], dp=there)

    def w_cut_send():
        loads[9].wait()

        @pl.when(me == w_src)
        def _():
            w_cut[...] = jnp.zeros(w_cut.shape, BF)
            for q in range(2 * nx):
                w_cut[q, 0:ddw_v.shape[0], 0:feat] = ddw_v[:, q * feat:(q + 1) * feat]
            for k in range(1, 2 * nx):
                w_x_copy(k).start()
            low, lanes = w_place(z)
            mine = pltpu.make_async_copy(w_cut.at[me, rows(low, w_half), lanes], w_part(z), wx_s.at[0])
            mine.start()
            mine.wait()

    def w_cut_recv():
        @pl.when(me != w_src)
        def _():
            w_x_copy(1).wait_recv()

    def w_z_copy(k, zz):
        return rdma(w_part(zz), w_part(zz), wz_s.at[k], wz_r.at[k], tensor=(z + k) % nz)

    def w_y_copy(d, hop, origin):
        low, size = (origin * 2 * hid_rows, 2 * hid_rows) if hop < ny // 2 else ((origin * 2 + d) * hid_rows, hid_rows)
        ref = w_all.at[rows(low, size), :]
        return rdma(ref, ref, wy_s.at[d, hop - 1], wy_r.at[d, hop - 1], expert=(y + 1 - 2 * d + ny) % ny)

    def w_y_step(hop):
        if hop > ny // 2:
            return
        for d in range(2):
            origin = (y - (1 - 2 * d) * hop + ny) % ny
            w_y_copy(d, hop, origin).wait_recv()
            if hop < ny // 2:
                go(w_y_copy(d, hop + 1, origin))

    for j in range(npair):
        expert_pair(j)
    w_cut_send()
    x_step(0, 1)
    q_recv(qe, qe_s, qe_r, 0)
    rs_open(eflow)
    x_step(1, 1)
    for j in range(1, npair):
        q_recv(qe, qe_s, qe_r, j)
    rs_open_1(eflow)
    x_step(0, 2)

    loads[5].wait()
    loads[6].wait()
    n_tok = routes_v.shape[1]
    lane = lax.broadcasted_iota(jnp.int32, (n_tok, n_tok), 1)
    row = lax.broadcasted_iota(jnp.int32, (n_tok, n_tok), 0)
    named = [routes_v[k:k + 1, :] for k in range(2)]
    hot = [jnp.where(row == named[k], 1.0, 0.0).astype(F32) for k in range(2)]
    earlier = jnp.where(row < lane, 1.0, 0.0).astype(BF)
    count = jnp.dot((hot[0] + hot[1]).astype(BF), earlier, preferred_element_type=F32)
    place_s = lax.broadcasted_iota(jnp.int32, (slots, n_tok), 0).astype(F32)
    weighing = jnp.zeros((slots, n_tok), F32)
    for k in range(2):
        rank = jnp.sum(count * hot[k], axis=0, keepdims=True)
        place = ((named[k] % nz) * (ny * cap) + (named[k] // nz) * cap).astype(F32) + rank
        weighing = weighing + jnp.where(place_s == place, scores_v[k:k + 1, :], 0.0)
    high = weighing.astype(BF)
    whi[...] = high
    wlo[...] = (weighing - high.astype(F32)).astype(BF)
    row_s = lax.broadcasted_iota(jnp.int32, (slots, slots), 0)
    lane_t = lax.broadcasted_iota(jnp.int32, (slots, slots), 1)
    i_s = lax.broadcasted_iota(jnp.int32, (slots, 1), 0)
    j_s = ((i_s % (ny * cap)) // cap) * (nz * cap) + (i_s // (ny * cap)) * cap + i_s % cap
    perm[...] = jnp.where(lane_t == j_s, 1.0, 0.0).astype(BF)

    rs_step(eflow, 1, False)
    x_step(1, 2)
    rs_step(eflow, 2, True)
    x_step(0, 3)
    rs_step(eflow, 2, False)
    w_cut_recv()
    meet_y_z()
    for k in range(1, nz):
        go(w_z_copy(k, z))
    x_step(1, 3)
    rs_step(eflow, 3, True)
    x_step(0, 4)

    def hidden_part(t):
        x_finish(t)
        block = x_all[:, t * part:(t + 1) * part]
        gate = jnp.dot(dgw_v[...], block, preferred_element_type=F32)
        up = jnp.dot(duw_v[...], block, preferred_element_type=F32)
        hidden = gate * jax.nn.sigmoid(gate) * up
        hidden = jnp.concatenate([hidden, jnp.zeros((hid_rows - hidden.shape[0], part), F32)], axis=0)
        h_all[rows(me * hid_rows, hid_rows), t * part:(t + 1) * part] = hidden.astype(BF)
        for copy in h_first(t):
            go(copy)

    def dense_part(t):
        h_finish(t)
        block = h_all[:, t * part:(t + 1) * part]
        out = lax.dot_general(w_all[...], block, TN, preferred_element_type=F32)
        dense_o[:, t * part:(t + 1) * part] = out[:feat, :].astype(BF)

    own_x.wait()
    for i in range(7, 9):
        loads[i].wait()
    hidden_part(0)
    for k in range(1, nz):
        w_z_copy(k, (z - k + nz) % nz).wait_recv()
    if ny > 1:
        for d in range(2):
            go(w_y_copy(d, 1, y))
    rs_step(eflow, 3, False)
    x_step(1, 4)
    hidden_part(1)
    w_y_step(1)
    h_step(0, 1)

    ef_v[pl.ds(2 * half, ef_v.shape[0] - 2 * half), :] = jnp.zeros((ef_v.shape[0] - 2 * half, slots), BF)
    for h in range(2):
        ef_v[pl.ds(h * half, half), :] = rs_final(eflow, h)
    eye = jnp.where(lane_t == row_s, 1.0, 0.0).astype(BF)
    a1[...] = lax.dot_general(eye, ef_v[...], NT, preferred_element_type=F32).astype(BF)
    ny_rows, nz_rows = nz * cap, ny * cap

    def y_copy(k):
        return rdma(
            a1.at[rows((y + k) % ny * ny_rows, ny_rows), :], a2.at[rows(y * ny_rows, ny_rows), :],
            y_s.at[k], y_r.at[k], expert=(y + k) % ny,
        )

    def z_copy(k):
        return rdma(
            a3.at[rows((z + k) % nz * nz_rows, nz_rows), :], a4.at[rows(z * nz_rows, nz_rows), :],
            z_s.at[k], z_r.at[k], tensor=(z + k) % nz,
        )

    def y_wait(k):
        ref = a2.at[rows((y - k + ny) % ny * ny_rows, ny_rows), :]
        rdma(ref, ref, y_s.at[k], y_r.at[k], expert=(y + k) % ny).wait_recv()

    def z_wait(k):
        ref = a4.at[rows((z - k + nz) % nz * nz_rows, nz_rows), :]
        rdma(ref, ref, z_s.at[k], z_r.at[k], tensor=(z + k) % nz).wait_recv()

    for k in range(1, ny):
        go(y_copy(k))
    a2[rows(y * ny_rows, ny_rows), :] = a1[rows(y * ny_rows, ny_rows), :]
    h_step(1, 1)
    w_y_step(2)
    h_step(0, 2)
    for k in range(1, ny):
        y_wait(k)
    a3[...] = jnp.dot(perm[...], a2[...], preferred_element_type=F32).astype(BF)
    for k in range(1, nz):
        go(z_copy(k))
    a4[rows(z * nz_rows, nz_rows), :] = a3[rows(z * nz_rows, nz_rows), :]
    h_step(1, 2)
    w_y_step(3)
    h_step(0, 3)
    h_step(1, 3)
    w_y_step(4)
    h_step(0, 4)
    h_step(1, 4)
    for t in range(2):
        dense_part(t)
    for k in range(1, nz):
        z_wait(k)
    mixed = lax.dot_general(a4[...], whi[...], TN, preferred_element_type=F32)
    mixed = mixed + lax.dot_general(a4[...], wlo[...], TN, preferred_element_type=F32)
    grad_o[...] = mixed[:feat, :].astype(BF)

    @pl.when(me == w_src)
    def _():
        for k in range(1, 2 * nx):
            w_x_copy(k).wait_send()

    for copy in pending:
        copy.wait_send()


def local(ny, nz, routes, gate_scores, back_hidden, saved_gate, saved_up, egw, euw, inputs_b, dgw, duw, ddw):
    feat, toks = inputs_b.shape
    hid, model = dgw.shape
    slots = back_hidden.shape[2]
    n_tok = routes.shape[0]
    nx = model // feat // 2
    far = nx // 2
    cap = slots // (ny * nz)
    half = feat // 2
    part = toks // 2
    hid_rows = -(-hid // 32) * 32
    wide = -(-feat // 128) * 128
    steps = 2 * far - 1
    vm, dma = pltpu.VMEM, pltpu.SemaphoreType.DMA
    scratch = [
        vm((2, n_tok), jnp.int32), vm((2, n_tok), F32),
        vm((hid, slots), BF), vm((hid, slots), BF), vm((hid, slots), BF),
        vm((hid, model), BF), vm((hid, model), BF), vm((hid, model), BF), vm((hid, model), BF), vm((hid, model), BF),
        vm((model, toks), BF), vm((2 * nx * hid_rows, toks), BF), vm((2 * nx * hid_rows, wide), BF), vm((2 * nx, hid_rows, wide), BF),
        vm((model, slots), BF), vm((model // 2, slots), BF),
        vm((2, steps, half, slots), BF), vm((2, steps, half, slots), BF),
        vm((hid, slots), BF), vm((hid, slots), BF), vm((wide, slots), BF),
        vm((slots, wide), BF), vm((slots, wide), BF), vm((slots, wide), BF), vm((slots, wide), BF),
        vm((slots, n_tok), BF), vm((slots, n_tok), BF), vm((slots, slots), BF),
        pltpu.SemaphoreType.REGULAR((3,)), dma((11,)),
        dma((2, 2, far, 2)), dma((2, 2, far, 2)), dma((2, 1 + 4 * far)), dma((2, 1 + 4 * far)),
        dma((2, 2, far, 2)), dma((2, 2, far, 2)), dma((2, 1 + 4 * far)), dma((2, 1 + 4 * far)),
        dma((2 * nx,)), dma((1,)), dma((nz,)), dma((nz,)), dma((2, max(1, ny // 2))), dma((2, max(1, ny // 2))),
        dma((nx,)), dma((nx,)),
        dma((2, steps)), dma((2, steps)),
        dma((ny,)), dma((ny,)), dma((nz,)), dma((nz,)),
    ]
    return pl.pallas_call(
        functools.partial(kernel, nx, ny, nz, cap),
        out_shape=(pltpu.VMEM((feat, n_tok), BF), pltpu.VMEM((feat, toks), BF)),
        in_specs=[pl.BlockSpec(memory_space=pltpu.HBM)] * 11,
        out_specs=(pl.BlockSpec(memory_space=pltpu.VMEM), pl.BlockSpec(memory_space=pltpu.VMEM)),
        scratch_shapes=scratch,
        compiler_params=pltpu.CompilerParams(
            collective_id=0, has_side_effects=True, vmem_limit_bytes=62 * 1024 * 1024
        ),
    )(routes.T, gate_scores.T, back_hidden, saved_gate, saved_up, egw, euw, inputs_b, dgw, duw, ddw)


def solution(mesh):
    both = ("expert", "tensor")
    in_specs = (
        P(both, None), P(both, None),
        P(both, "dp", None), P(both, "dp", None), P(both, "dp", None), P(both, "dp", None), P(both, "dp", None),
        P("dp", both), P("dp", None), P("dp", None), P("dp", None),
    )
    out_specs = (P("dp", both), P("dp", both))
    body = functools.partial(local, mesh.shape["expert"], mesh.shape["tensor"])
    return jax.shard_map(body, mesh=mesh, in_specs=in_specs, out_specs=out_specs, check_vma=False)
```

```python
import functools

import jax
import jax.numpy as jnp
from jax import lax
from jax.experimental import pallas as pl
from jax.experimental.pallas import tpu as pltpu
from jax.sharding import PartitionSpec as P

MESH = pl.DeviceIdType.MESH
BF = jnp.bfloat16
F32 = jnp.float32
TN = (((0,), (0,)), ((), ()))
NT = (((1,), (1,)), ((), ()))


def kernel(
    nx, ny, nz, cap,
    routes_h, scores_h, back_h, sgate_h, sup_h, egw_h, euw_h, inb_h, dgw_h, duw_h, ddw_h,
    grad_o, dense_o,
    routes_v, scores_v, back_v, sgate_v, sup_v, egw_v, euw_v, dgw_v, duw_v, ddw_v,
    x_all, pe, qe, pd, qd, se, re, sd, rd,
    gg_v, gu_v, ef_v, a1, a2, a3, a4, whi, wlo, perm,
    meet, load_sem, ag_s, ag_r, sib_s, sib_r, qe_s, qe_r, qd_s, qd_r, se_s, re_s, sd_s, rd_s, y_s, y_r, z_s, z_r,
):
    feat = inb_h.shape[0]
    half = feat // 2
    slots = back_h.shape[2]
    part = inb_h.shape[1] // 2
    pair = 4 * feat
    npair = nx // 2
    far = nx // 2
    me = lax.axis_index("dp")
    x, c = me // 2, me % 2
    y, z = lax.axis_index("expert"), lax.axis_index("tensor")
    sib = x * 2 + 1 - c

    def chip(offset):
        return (x + offset + nx) % nx

    def dp_of(offset):
        return chip(offset) * 2 + c

    def rdma(src, dst, ssem, rsem, **where):
        return pltpu.make_async_remote_copy(
            src_ref=src, dst_ref=dst, send_sem=ssem, recv_sem=rsem, device_id=where, device_id_type=MESH
        )

    def rows(start, size):
        return pl.ds(pl.multiple_of(start, 16), size)

    loads = []
    sources = (sgate_h.at[0], back_h.at[0], sup_h.at[0], egw_h.at[0], euw_h.at[0], routes_h, scores_h, dgw_h, duw_h, ddw_h)
    targets = (sgate_v, back_v, sup_v, egw_v, euw_v, routes_v, scores_v, dgw_v, duw_v, ddw_v)
    for i, (src, dst) in enumerate(zip(sources, targets)):
        loads.append(pltpu.make_async_copy(src, dst, load_sem.at[i]))
    own_x = pltpu.make_async_copy(inb_h, x_all.at[rows(me * feat, feat), :], load_sem.at[len(sources)])
    own_x.start()
    for load in loads:
        load.start()

    def x_part(dp, t, h, size):
        return x_all.at[rows(dp * feat + h * half, size), pl.ds(t * part, part)]

    def ag_copy(d, t, hop, h, origin):
        src = dst = x_part(origin, t, h, half)
        if hop == 1:
            src = inb_h.at[pl.ds(h * half, half), pl.ds(t * part, part)]
        return rdma(src, dst, ag_s.at[t, d, hop - 1, h], ag_r.at[t, d, hop - 1, h], dp=dp_of(1 - 2 * d))

    def sib_copy(t, slot, h, origin, size):
        src = dst = x_part(origin, t, h, size)
        if slot == 0:
            src = inb_h.at[:, pl.ds(t * part, part)]
        return rdma(src, dst, sib_s.at[t, slot], sib_r.at[t, slot], dp=sib)

    def ag_open():
        copies = []
        for t in range(2):
            copies += [ag_copy(d, t, 1, h, me) for h in range(2) for d in range(2)]
            copies.append(sib_copy(t, 0, 0, me, feat))
        return copies

    def ag_step(t, hop):
        for h in range(2):
            for d in range(2):
                if hop == far and h != d:
                    continue
                origin = dp_of(-(1 - 2 * d) * hop)
                ag_copy(d, t, hop, h, origin).wait_recv()
                if hop + 1 < far or (hop + 1 == far and h == d):
                    go(ag_copy(d, t, hop + 1, h, origin))
                go(sib_copy(t, 1 + (hop - 1) * 4 + d * 2 + h, h, origin, half))

    def sib_wait(t):
        sib_copy(t, 0, 0, sib, feat).wait_recv()
        for hop in range(1, far + 1):
            for h in range(2):
                for d in range(2):
                    if hop < far or h == d:
                        origin = chip(-(1 - 2 * d) * hop) * 2 + 1 - c
                        sib_copy(t, 1 + (hop - 1) * 4 + d * 2 + h, h, origin, half).wait_recv()

    barrier = pltpu.get_barrier_semaphore()
    y_z = [dict(expert=(y + k) % ny) for k in range(1, ny)]
    y_z += [dict(tensor=(z + k) % nz) for k in range(1, nz)]

    def signal(sem, **where):
        pl.semaphore_signal(sem, inc=1, device_id=where, device_id_type=MESH)

    @pl.when(c == 0)
    def _():
        signal(barrier, dp=dp_of(1))
        signal(barrier, dp=dp_of(-1))
        pl.semaphore_wait(barrier, 3)
        signal(meet.at[0], dp=dp_of(1))
        signal(meet.at[0], dp=dp_of(-1))
        for copy in ag_open():
            copy.start()
        pl.semaphore_wait(meet.at[0], 2)
        signal(meet.at[1], dp=sib)

    @pl.when(c == 1)
    def _():
        signal(barrier, dp=sib)
        pl.semaphore_wait(meet.at[1], 1)
        for copy in ag_open():
            copy.start()
        for where in y_z:
            signal(barrier, **where)

    def meet_y_z():
        @pl.when(c == 1)
        def _():
            if y_z:
                pl.semaphore_wait(barrier, len(y_z))
            signal(meet.at[2], dp=sib)

        @pl.when(c == 0)
        def _():
            pl.semaphore_wait(meet.at[2], 1)

    pending = []

    def go(copy):
        copy.start()
        pending.append(copy)

    pending.extend(ag_open())

    for i in range(3):
        loads[i].wait()
    gate_pre = sgate_v[...].astype(F32)
    back = back_v[...].astype(F32)
    sig = jax.nn.sigmoid(gate_pre)
    gg_v[...] = (back * sup_v[...].astype(F32) * sig * (1.0 + gate_pre * (1.0 - sig))).astype(BF)
    gu_v[...] = (back * gate_pre * sig).astype(BF)
    loads[3].wait()
    loads[4].wait()

    pair_order = [npair // 2] + [k for k in range(npair) if k not in (0, npair // 2)] + [0]

    def chip_pair(j):
        return (x // 2 + pair_order[j]) % npair

    def expert_pair(j):
        p = chip_pair(j)
        lanes = pl.ds(pl.multiple_of(p * pair, 128), pair)
        out = lax.dot_general(egw_v[:, lanes], gg_v[...], TN, preferred_element_type=F32)
        out = out + lax.dot_general(euw_v[:, lanes], gu_v[...], TN, preferred_element_type=F32)
        pe[rows(p * pair, pair), :] = out.astype(BF)
        for i in range(2):
            q_send(pe, qe, qe_s, qe_r, p * 2 + i, j * 2 + i)

    def q_rows(q, there):
        return q.at[rows(there * feat, feat), :]

    def q_send(p, q, ss, rs, there, slot):
        src = p.at[rows((there * 2 + 1 - c) * feat, feat), :]
        go(rdma(src, q_rows(q, there), ss.at[slot], rs.at[slot], dp=sib))

    def q_recv(q, ss, rs, j):
        for i in range(2):
            ref = q_rows(q, chip_pair(j) * 2 + i)
            rdma(ref, ref, ss.at[j * 2 + i], rs.at[j * 2 + i], dp=sib).wait_recv()

    def slot_of(hop, h):
        return 0 if hop == 0 else 1 + (hop - 1) * 2 + h

    def partial(p, q, there, h):
        own = p[rows((there * 2 + c) * feat + h * half, half), :].astype(F32)
        return own + q[rows(there * feat + h * half, half), :].astype(F32)

    def rs_copy(s, r, ss, rs, d, slot):
        return rdma(s.at[d, slot], r.at[d, slot], ss.at[d, slot], rs.at[d, slot], dp=dp_of(1 - 2 * d))

    def rs_send(flow, d, hop, h):
        p, q, s, r, ss, rs = flow
        slot = slot_of(hop, h)
        total = partial(p, q, chip((1 - 2 * d) * (far - hop)), h)
        if hop > 1 or (hop == 1 and h == d):
            before = slot_of(hop - 1, h)
            rs_copy(s, r, ss, rs, d, before).wait_recv()
            total = total + r[d, before].astype(F32)
        s[d, slot] = total.astype(BF)
        go(rs_copy(s, r, ss, rs, d, slot))

    def rs_open(flow):
        for d in range(2):
            rs_send(flow, d, 0, d)

    def rs_open_1(flow):
        for d in range(2):
            rs_send(flow, d, 1, 1 - d)

    def rs_step(flow, hop, other):
        for d in range(2):
            rs_send(flow, d, hop, 1 - d if other else d)

    def rs_final(flow, h):
        p, q, s, r, ss, rs = flow
        total = partial(p, q, x, h)
        for d in range(2):
            slot = slot_of(far - 1, h)
            rs_copy(s, r, ss, rs, d, slot).wait_recv()
            total = total + r[d, slot].astype(F32)
        return total.astype(BF)

    eflow = (pe, qe, se, re, se_s, re_s)
    dflow = [tuple(ref.at[t] for ref in (pd, qd, sd, rd, sd_s, rd_s)) for t in range(2)]

    for j in range(npair):
        expert_pair(j)
    for t in range(2):
        ag_step(t, 1)
    q_recv(qe, qe_s, qe_r, 0)
    rs_open(eflow)
    for j in range(1, npair):
        q_recv(qe, qe_s, qe_r, j)
    rs_open_1(eflow)

    loads[5].wait()
    loads[6].wait()
    n_tok = routes_v.shape[1]
    lane = lax.broadcasted_iota(jnp.int32, (n_tok, n_tok), 1)
    row = lax.broadcasted_iota(jnp.int32, (n_tok, n_tok), 0)
    named = [routes_v[k:k + 1, :] for k in range(2)]
    hot = [jnp.where(row == named[k], 1.0, 0.0).astype(F32) for k in range(2)]
    earlier = jnp.where(row < lane, 1.0, 0.0).astype(BF)
    count = jnp.dot((hot[0] + hot[1]).astype(BF), earlier, preferred_element_type=F32)
    place_s = lax.broadcasted_iota(jnp.int32, (slots, n_tok), 0).astype(F32)
    weighing = jnp.zeros((slots, n_tok), F32)
    for k in range(2):
        rank = jnp.sum(count * hot[k], axis=0, keepdims=True)
        place = ((named[k] % nz) * (ny * cap) + (named[k] // nz) * cap).astype(F32) + rank
        weighing = weighing + jnp.where(place_s == place, scores_v[k:k + 1, :], 0.0)
    high = weighing.astype(BF)
    whi[...] = high
    wlo[...] = (weighing - high.astype(F32)).astype(BF)
    row_s = lax.broadcasted_iota(jnp.int32, (slots, slots), 0)
    lane_t = lax.broadcasted_iota(jnp.int32, (slots, slots), 1)
    i_s = lax.broadcasted_iota(jnp.int32, (slots, 1), 0)
    j_s = ((i_s % (ny * cap)) // cap) * (nz * cap) + (i_s // (ny * cap)) * cap + i_s % cap
    perm[...] = jnp.where(lane_t == j_s, 1.0, 0.0).astype(BF)

    for t in range(2):
        ag_step(t, 2)
    for t in range(2):
        ag_step(t, 3)
    rs_step(eflow, 1, False)
    ag_step(0, 4)
    rs_step(eflow, 2, True)

    def dense_part(t):
        sib_wait(t)
        block = x_all[:, t * part:(t + 1) * part]
        gate = jnp.dot(dgw_v[...], block, preferred_element_type=F32)
        up = jnp.dot(duw_v[...], block, preferred_element_type=F32)
        hidden = (gate * jax.nn.sigmoid(gate) * up).astype(BF)
        p_t, q_t, ss, rs = pd.at[t], qd.at[t], qd_s.at[t], qd_r.at[t]
        for j in range(npair):
            p = chip_pair(j)
            lanes = pl.ds(pl.multiple_of(p * pair, 128), pair)
            out = lax.dot_general(ddw_v[:, lanes], hidden, TN, preferred_element_type=F32)
            p_t[rows(p * pair, pair), :] = out.astype(BF)
            for i in range(2):
                q_send(p_t, q_t, ss, rs, p * 2 + i, j * 2 + i)

    def dense_recv(t, j):
        q_recv(qd.at[t], qd_s.at[t], qd_r.at[t], j)

    own_x.wait()
    for i in range(7, 10):
        loads[i].wait()
    dense_part(0)
    ag_step(1, 4)
    rs_step(eflow, 2, False)
    dense_recv(0, 0)
    rs_open(dflow[0])
    dense_recv(0, 1)
    dense_recv(0, 2)
    rs_open_1(dflow[0])
    rs_step(eflow, 3, True)
    dense_part(1)
    rs_step(eflow, 3, False)
    dense_recv(1, 0)
    rs_open(dflow[1])
    dense_recv(1, 1)
    dense_recv(1, 2)
    rs_open_1(dflow[1])
    rs_step(dflow[0], 1, False)

    ef_v[pl.ds(2 * half, ef_v.shape[0] - 2 * half), :] = jnp.zeros((ef_v.shape[0] - 2 * half, slots), BF)
    for h in range(2):
        ef_v[pl.ds(h * half, half), :] = rs_final(eflow, h)
    eye = jnp.where(lane_t == row_s, 1.0, 0.0).astype(BF)
    a1[...] = lax.dot_general(eye, ef_v[...], NT, preferred_element_type=F32).astype(BF)
    ny_rows, nz_rows = nz * cap, ny * cap

    def y_copy(k):
        return rdma(
            a1.at[rows((y + k) % ny * ny_rows, ny_rows), :], a2.at[rows(y * ny_rows, ny_rows), :],
            y_s.at[k], y_r.at[k], expert=(y + k) % ny,
        )

    def z_copy(k):
        return rdma(
            a3.at[rows((z + k) % nz * nz_rows, nz_rows), :], a4.at[rows(z * nz_rows, nz_rows), :],
            z_s.at[k], z_r.at[k], tensor=(z + k) % nz,
        )

    def y_wait(k):
        ref = a2.at[rows((y - k + ny) % ny * ny_rows, ny_rows), :]
        rdma(ref, ref, y_s.at[k], y_r.at[k], expert=(y + k) % ny).wait_recv()

    def z_wait(k):
        ref = a4.at[rows((z - k + nz) % nz * nz_rows, nz_rows), :]
        rdma(ref, ref, z_s.at[k], z_r.at[k], tensor=(z + k) % nz).wait_recv()

    meet_y_z()
    for k in range(1, ny):
        go(y_copy(k))
    a2[rows(y * ny_rows, ny_rows), :] = a1[rows(y * ny_rows, ny_rows), :]
    rs_step(dflow[1], 1, False)
    rs_step(dflow[0], 2, True)
    rs_step(dflow[0], 2, False)
    for k in range(1, ny):
        y_wait(k)
    a3[...] = jnp.dot(perm[...], a2[...], preferred_element_type=F32).astype(BF)
    for k in range(1, nz):
        go(z_copy(k))
    a4[rows(z * nz_rows, nz_rows), :] = a3[rows(z * nz_rows, nz_rows), :]
    rs_step(dflow[1], 2, True)
    rs_step(dflow[1], 2, False)
    dense_recv(0, 3)
    dense_recv(1, 3)
    rs_step(dflow[0], 3, True)
    rs_step(dflow[0], 3, False)
    rs_step(dflow[1], 3, True)
    rs_step(dflow[1], 3, False)
    for t in range(2):
        for h in range(2):
            dense_o[pl.ds(h * half, half), pl.ds(t * part, part)] = rs_final(dflow[t], h)
    for k in range(1, nz):
        z_wait(k)
    mixed = lax.dot_general(a4[...], whi[...], TN, preferred_element_type=F32)
    mixed = mixed + lax.dot_general(a4[...], wlo[...], TN, preferred_element_type=F32)
    grad_o[...] = mixed[:feat, :].astype(BF)
    for copy in pending:
        copy.wait_send()


def local(ny, nz, routes, gate_scores, back_hidden, saved_gate, saved_up, egw, euw, inputs_b, dgw, duw, ddw):
    feat, toks = inputs_b.shape
    hid, model = dgw.shape
    slots = back_hidden.shape[2]
    n_tok = routes.shape[0]
    nx = model // feat // 2
    far = nx // 2
    cap = slots // (ny * nz)
    half = feat // 2
    part = toks // 2
    wide = -(-feat // 128) * 128
    steps = 2 * far - 1
    vm, dma = pltpu.VMEM, pltpu.SemaphoreType.DMA
    scratch = [
        vm((2, n_tok), jnp.int32), vm((2, n_tok), F32),
        vm((hid, slots), BF), vm((hid, slots), BF), vm((hid, slots), BF),
        vm((hid, model), BF), vm((hid, model), BF), vm((hid, model), BF), vm((hid, model), BF), vm((hid, model), BF),
        vm((model, toks), BF),
        vm((model, slots), BF), vm((model // 2, slots), BF), vm((2, model, part), BF), vm((2, model // 2, part), BF),
        vm((2, steps, half, slots), BF), vm((2, steps, half, slots), BF),
        vm((2, 2, steps, half, part), BF), vm((2, 2, steps, half, part), BF),
        vm((hid, slots), BF), vm((hid, slots), BF), vm((wide, slots), BF),
        vm((slots, wide), BF), vm((slots, wide), BF), vm((slots, wide), BF), vm((slots, wide), BF),
        vm((slots, n_tok), BF), vm((slots, n_tok), BF), vm((slots, slots), BF),
        pltpu.SemaphoreType.REGULAR((3,)), dma((11,)),
        dma((2, 2, far, 2)), dma((2, 2, far, 2)), dma((2, 1 + 4 * far)), dma((2, 1 + 4 * far)),
        dma((nx,)), dma((nx,)), dma((2, nx)), dma((2, nx)),
        dma((2, steps)), dma((2, steps)), dma((2, 2, steps)), dma((2, 2, steps)),
        dma((ny,)), dma((ny,)), dma((nz,)), dma((nz,)),
    ]
    return pl.pallas_call(
        functools.partial(kernel, nx, ny, nz, cap),
        out_shape=(pltpu.VMEM((feat, n_tok), BF), pltpu.VMEM((feat, toks), BF)),
        in_specs=[pl.BlockSpec(memory_space=pltpu.HBM)] * 11,
        out_specs=(pl.BlockSpec(memory_space=pltpu.VMEM), pl.BlockSpec(memory_space=pltpu.VMEM)),
        scratch_shapes=scratch,
        compiler_params=pltpu.CompilerParams(
            collective_id=0, has_side_effects=True, vmem_limit_bytes=62 * 1024 * 1024
        ),
    )(routes.T, gate_scores.T, back_hidden, saved_gate, saved_up, egw, euw, inputs_b, dgw, duw, ddw)


def solution(mesh):
    both = ("expert", "tensor")
    in_specs = (
        P(both, None), P(both, None),
        P(both, "dp", None), P(both, "dp", None), P(both, "dp", None), P(both, "dp", None), P(both, "dp", None),
        P("dp", both), P("dp", None), P("dp", None), P("dp", None),
    )
    out_specs = (P("dp", both), P("dp", both))
    body = functools.partial(local, mesh.shape["expert"], mesh.shape["tensor"])
    return jax.shard_map(body, mesh=mesh, in_specs=in_specs, out_specs=out_specs, check_vma=False)
```

```python
import functools

import jax
import jax.numpy as jnp
from jax import lax
from jax.experimental import pallas as pl
from jax.experimental.pallas import tpu as pltpu
from jax.sharding import PartitionSpec as P

MESH = pl.DeviceIdType.MESH
BF = jnp.bfloat16
F32 = jnp.float32
TN = (((0,), (0,)), ((), ()))
NT = (((1,), (1,)), ((), ()))


def kernel(
    nx, ny, nz, cap,
    routes_h, scores_h, back_h, sgate_h, sup_h, egw_h, euw_h, inb_h, dgw_h, duw_h, ddw_h,
    grad_o, dense_o,
    routes_v, scores_v, back_v, sgate_v, sup_v, egw_v, euw_v, dgw_v, duw_v, ddw_v,
    x_all, pe, qe, pd, qd, se, re, sd, rd,
    gg_v, gu_v, ef_v, a1, a2, a3, a4, whi, wlo, perm,
    meet, load_sem, ag_s, ag_r, sib_s, sib_r, qe_s, qe_r, qd_s, qd_r, se_s, re_s, sd_s, rd_s, y_s, y_r, z_s, z_r,
):
    feat = inb_h.shape[0]
    half = feat // 2
    slots = back_h.shape[2]
    part = inb_h.shape[1] // 2
    pair = 4 * feat
    npair = nx // 2
    far = nx // 2
    me = lax.axis_index("dp")
    x, c = me // 2, me % 2
    y, z = lax.axis_index("expert"), lax.axis_index("tensor")
    sib = x * 2 + 1 - c

    def chip(offset):
        return (x + offset + nx) % nx

    def dp_of(offset):
        return chip(offset) * 2 + c

    def rdma(src, dst, ssem, rsem, **where):
        return pltpu.make_async_remote_copy(
            src_ref=src, dst_ref=dst, send_sem=ssem, recv_sem=rsem, device_id=where, device_id_type=MESH
        )

    def rows(start, size):
        return pl.ds(pl.multiple_of(start, 16), size)

    loads = []
    sources = (sgate_h.at[0], back_h.at[0], sup_h.at[0], egw_h.at[0], euw_h.at[0], routes_h, scores_h, dgw_h, duw_h, ddw_h)
    targets = (sgate_v, back_v, sup_v, egw_v, euw_v, routes_v, scores_v, dgw_v, duw_v, ddw_v)
    for i, (src, dst) in enumerate(zip(sources, targets)):
        loads.append(pltpu.make_async_copy(src, dst, load_sem.at[i]))
    own_x = pltpu.make_async_copy(inb_h, x_all.at[rows(me * feat, feat), :], load_sem.at[len(sources)])
    own_x.start()
    for load in loads:
        load.start()

    def x_part(dp, t, h, size):
        return x_all.at[rows(dp * feat + h * half, size), pl.ds(t * part, part)]

    def ag_copy(d, t, hop, h, origin):
        src = dst = x_part(origin, t, h, half)
        if hop == 1:
            src = inb_h.at[pl.ds(h * half, half), pl.ds(t * part, part)]
        return rdma(src, dst, ag_s.at[t, d, hop - 1, h], ag_r.at[t, d, hop - 1, h], dp=dp_of(1 - 2 * d))

    def sib_copy(t, slot, h, origin, size):
        src = dst = x_part(origin, t, h, size)
        if slot == 0:
            src = inb_h.at[:, pl.ds(t * part, part)]
        return rdma(src, dst, sib_s.at[t, slot], sib_r.at[t, slot], dp=sib)

    def ag_open():
        copies = []
        for t in range(2):
            copies += [ag_copy(d, t, 1, h, me) for h in range(2) for d in range(2)]
            copies.append(sib_copy(t, 0, 0, me, feat))
        return copies

    def ag_step(t, hop):
        for h in range(2):
            for d in range(2):
                if hop == far and h != d:
                    continue
                origin = dp_of(-(1 - 2 * d) * hop)
                ag_copy(d, t, hop, h, origin).wait_recv()
                if hop + 1 < far or (hop + 1 == far and h == d):
                    go(ag_copy(d, t, hop + 1, h, origin))
                go(sib_copy(t, 1 + (hop - 1) * 4 + d * 2 + h, h, origin, half))

    def sib_wait(t):
        sib_copy(t, 0, 0, sib, feat).wait_recv()
        for hop in range(1, far + 1):
            for h in range(2):
                for d in range(2):
                    if hop < far or h == d:
                        origin = chip(-(1 - 2 * d) * hop) * 2 + 1 - c
                        sib_copy(t, 1 + (hop - 1) * 4 + d * 2 + h, h, origin, half).wait_recv()

    barrier = pltpu.get_barrier_semaphore()
    y_z = [dict(expert=(y + k) % ny) for k in range(1, ny)]
    y_z += [dict(tensor=(z + k) % nz) for k in range(1, nz)]

    def signal(sem, **where):
        pl.semaphore_signal(sem, inc=1, device_id=where, device_id_type=MESH)

    @pl.when(c == 0)
    def _():
        signal(barrier, dp=dp_of(1))
        signal(barrier, dp=dp_of(-1))
        pl.semaphore_wait(barrier, 3)
        signal(meet.at[0], dp=dp_of(1))
        signal(meet.at[0], dp=dp_of(-1))
        for copy in ag_open():
            copy.start()
        pl.semaphore_wait(meet.at[0], 2)
        signal(meet.at[1], dp=sib)

    @pl.when(c == 1)
    def _():
        signal(barrier, dp=sib)
        pl.semaphore_wait(meet.at[1], 1)
        for copy in ag_open():
            copy.start()
        for where in y_z:
            signal(barrier, **where)

    def meet_y_z():
        @pl.when(c == 1)
        def _():
            if y_z:
                pl.semaphore_wait(barrier, len(y_z))
            signal(meet.at[2], dp=sib)

        @pl.when(c == 0)
        def _():
            pl.semaphore_wait(meet.at[2], 1)

    pending = []

    def go(copy):
        copy.start()
        pending.append(copy)

    pending.extend(ag_open())

    for i in range(3):
        loads[i].wait()
    gate_pre = sgate_v[...].astype(F32)
    back = back_v[...].astype(F32)
    sig = jax.nn.sigmoid(gate_pre)
    gg_v[...] = (back * sup_v[...].astype(F32) * sig * (1.0 + gate_pre * (1.0 - sig))).astype(BF)
    gu_v[...] = (back * gate_pre * sig).astype(BF)
    loads[3].wait()
    loads[4].wait()

    pair_order = [npair // 2] + [k for k in range(npair) if k not in (0, npair // 2)] + [0]

    def chip_pair(j):
        return (x // 2 + pair_order[j]) % npair

    def expert_pair(j):
        p = chip_pair(j)
        lanes = pl.ds(pl.multiple_of(p * pair, 128), pair)
        out = lax.dot_general(egw_v[:, lanes], gg_v[...], TN, preferred_element_type=F32)
        out = out + lax.dot_general(euw_v[:, lanes], gu_v[...], TN, preferred_element_type=F32)
        pe[rows(p * pair, pair), :] = out.astype(BF)
        for i in range(2):
            q_send(pe, qe, qe_s, qe_r, p * 2 + i, j * 2 + i)

    def q_rows(q, there):
        return q.at[rows(there * feat, feat), :]

    def q_send(p, q, ss, rs, there, slot):
        src = p.at[rows((there * 2 + 1 - c) * feat, feat), :]
        go(rdma(src, q_rows(q, there), ss.at[slot], rs.at[slot], dp=sib))

    def q_recv(q, ss, rs, j):
        for i in range(2):
            ref = q_rows(q, chip_pair(j) * 2 + i)
            rdma(ref, ref, ss.at[j * 2 + i], rs.at[j * 2 + i], dp=sib).wait_recv()

    def slot_of(hop, h):
        return 0 if hop == 0 else 1 + (hop - 1) * 2 + h

    def partial(p, q, there, h):
        own = p[rows((there * 2 + c) * feat + h * half, half), :].astype(F32)
        return own + q[rows(there * feat + h * half, half), :].astype(F32)

    def rs_copy(s, r, ss, rs, d, slot):
        return rdma(s.at[d, slot], r.at[d, slot], ss.at[d, slot], rs.at[d, slot], dp=dp_of(1 - 2 * d))

    def rs_send(flow, d, hop, h):
        p, q, s, r, ss, rs = flow
        slot = slot_of(hop, h)
        total = partial(p, q, chip((1 - 2 * d) * (far - hop)), h)
        if hop > 1 or (hop == 1 and h == d):
            before = slot_of(hop - 1, h)
            rs_copy(s, r, ss, rs, d, before).wait_recv()
            total = total + r[d, before].astype(F32)
        s[d, slot] = total.astype(BF)
        go(rs_copy(s, r, ss, rs, d, slot))

    def rs_open(flow):
        for d in range(2):
            rs_send(flow, d, 0, d)

    def rs_open_1(flow):
        for d in range(2):
            rs_send(flow, d, 1, 1 - d)

    def rs_step(flow, hop, other):
        for d in range(2):
            rs_send(flow, d, hop, 1 - d if other else d)

    def rs_final(flow, h):
        p, q, s, r, ss, rs = flow
        total = partial(p, q, x, h)
        for d in range(2):
            slot = slot_of(far - 1, h)
            rs_copy(s, r, ss, rs, d, slot).wait_recv()
            total = total + r[d, slot].astype(F32)
        return total.astype(BF)

    eflow = (pe, qe, se, re, se_s, re_s)
    dflow = [tuple(ref.at[t] for ref in (pd, qd, sd, rd, sd_s, rd_s)) for t in range(2)]

    for j in range(npair):
        expert_pair(j)
    for t in range(2):
        ag_step(t, 1)
    q_recv(qe, qe_s, qe_r, 0)
    rs_open(eflow)
    for j in range(1, npair):
        q_recv(qe, qe_s, qe_r, j)
    rs_open_1(eflow)

    loads[5].wait()
    loads[6].wait()
    n_tok = routes_v.shape[1]
    lane = lax.broadcasted_iota(jnp.int32, (n_tok, n_tok), 1)
    row = lax.broadcasted_iota(jnp.int32, (n_tok, n_tok), 0)
    named = [routes_v[k:k + 1, :] for k in range(2)]
    hot = [jnp.where(row == named[k], 1.0, 0.0).astype(F32) for k in range(2)]
    earlier = jnp.where(row < lane, 1.0, 0.0).astype(BF)
    count = jnp.dot((hot[0] + hot[1]).astype(BF), earlier, preferred_element_type=F32)
    place_s = lax.broadcasted_iota(jnp.int32, (slots, n_tok), 0).astype(F32)
    weighing = jnp.zeros((slots, n_tok), F32)
    for k in range(2):
        rank = jnp.sum(count * hot[k], axis=0, keepdims=True)
        place = ((named[k] % nz) * (ny * cap) + (named[k] // nz) * cap).astype(F32) + rank
        weighing = weighing + jnp.where(place_s == place, scores_v[k:k + 1, :], 0.0)
    high = weighing.astype(BF)
    whi[...] = high
    wlo[...] = (weighing - high.astype(F32)).astype(BF)
    row_s = lax.broadcasted_iota(jnp.int32, (slots, slots), 0)
    lane_t = lax.broadcasted_iota(jnp.int32, (slots, slots), 1)
    i_s = lax.broadcasted_iota(jnp.int32, (slots, 1), 0)
    j_s = ((i_s % (ny * cap)) // cap) * (nz * cap) + (i_s // (ny * cap)) * cap + i_s % cap
    perm[...] = jnp.where(lane_t == j_s, 1.0, 0.0).astype(BF)

    for t in range(2):
        ag_step(t, 2)
    for t in range(2):
        ag_step(t, 3)
    rs_step(eflow, 1, False)
    ag_step(0, 4)
    rs_step(eflow, 2, True)

    def dense_part(t):
        sib_wait(t)
        block = x_all[:, t * part:(t + 1) * part]
        gate = jnp.dot(dgw_v[...], block, preferred_element_type=F32)
        up = jnp.dot(duw_v[...], block, preferred_element_type=F32)
        hidden = (gate * jax.nn.sigmoid(gate) * up).astype(BF)
        p_t, q_t, ss, rs = pd.at[t], qd.at[t], qd_s.at[t], qd_r.at[t]
        for j in range(npair):
            p = chip_pair(j)
            lanes = pl.ds(pl.multiple_of(p * pair, 128), pair)
            out = lax.dot_general(ddw_v[:, lanes], hidden, TN, preferred_element_type=F32)
            p_t[rows(p * pair, pair), :] = out.astype(BF)
            for i in range(2):
                q_send(p_t, q_t, ss, rs, p * 2 + i, j * 2 + i)

    def dense_recv(t, j):
        q_recv(qd.at[t], qd_s.at[t], qd_r.at[t], j)

    own_x.wait()
    for i in range(7, 10):
        loads[i].wait()
    dense_part(0)
    ag_step(1, 4)
    rs_step(eflow, 2, False)
    dense_recv(0, 0)
    rs_open(dflow[0])
    dense_recv(0, 1)
    dense_recv(0, 2)
    rs_open_1(dflow[0])
    rs_step(eflow, 3, True)
    dense_part(1)
    rs_step(eflow, 3, False)
    dense_recv(1, 0)
    rs_open(dflow[1])
    dense_recv(1, 1)
    dense_recv(1, 2)
    rs_open_1(dflow[1])
    rs_step(dflow[0], 1, False)

    ef_v[pl.ds(2 * half, ef_v.shape[0] - 2 * half), :] = jnp.zeros((ef_v.shape[0] - 2 * half, slots), BF)
    for h in range(2):
        ef_v[pl.ds(h * half, half), :] = rs_final(eflow, h)
    eye = jnp.where(lane_t == row_s, 1.0, 0.0).astype(BF)
    a1[...] = lax.dot_general(eye, ef_v[...], NT, preferred_element_type=F32).astype(BF)
    ny_rows, nz_rows = nz * cap, ny * cap

    def y_copy(k):
        return rdma(
            a1.at[rows((y + k) % ny * ny_rows, ny_rows), :], a2.at[rows(y * ny_rows, ny_rows), :],
            y_s.at[k], y_r.at[k], expert=(y + k) % ny,
        )

    def z_copy(k):
        return rdma(
            a3.at[rows((z + k) % nz * nz_rows, nz_rows), :], a4.at[rows(z * nz_rows, nz_rows), :],
            z_s.at[k], z_r.at[k], tensor=(z + k) % nz,
        )

    def y_wait(k):
        ref = a2.at[rows((y - k + ny) % ny * ny_rows, ny_rows), :]
        rdma(ref, ref, y_s.at[k], y_r.at[k], expert=(y + k) % ny).wait_recv()

    def z_wait(k):
        ref = a4.at[rows((z - k + nz) % nz * nz_rows, nz_rows), :]
        rdma(ref, ref, z_s.at[k], z_r.at[k], tensor=(z + k) % nz).wait_recv()

    meet_y_z()
    for k in range(1, ny):
        go(y_copy(k))
    a2[rows(y * ny_rows, ny_rows), :] = a1[rows(y * ny_rows, ny_rows), :]
    rs_step(dflow[1], 1, False)
    rs_step(dflow[0], 2, True)
    rs_step(dflow[0], 2, False)
    rs_step(dflow[1], 2, True)
    rs_step(dflow[1], 2, False)
    dense_recv(0, 3)
    dense_recv(1, 3)
    rs_step(dflow[0], 3, True)
    rs_step(dflow[0], 3, False)
    for k in range(1, ny):
        y_wait(k)
    a3[...] = jnp.dot(perm[...], a2[...], preferred_element_type=F32).astype(BF)
    for k in range(1, nz):
        go(z_copy(k))
    a4[rows(z * nz_rows, nz_rows), :] = a3[rows(z * nz_rows, nz_rows), :]
    rs_step(dflow[1], 3, True)
    rs_step(dflow[1], 3, False)
    for t in range(2):
        for h in range(2):
            dense_o[pl.ds(h * half, half), pl.ds(t * part, part)] = rs_final(dflow[t], h)
    for k in range(1, nz):
        z_wait(k)
    mixed = lax.dot_general(a4[...], whi[...], TN, preferred_element_type=F32)
    mixed = mixed + lax.dot_general(a4[...], wlo[...], TN, preferred_element_type=F32)
    grad_o[...] = mixed[:feat, :].astype(BF)
    for copy in pending:
        copy.wait_send()


def local(ny, nz, routes, gate_scores, back_hidden, saved_gate, saved_up, egw, euw, inputs_b, dgw, duw, ddw):
    feat, toks = inputs_b.shape
    hid, model = dgw.shape
    slots = back_hidden.shape[2]
    n_tok = routes.shape[0]
    nx = model // feat // 2
    far = nx // 2
    cap = slots // (ny * nz)
    half = feat // 2
    part = toks // 2
    wide = -(-feat // 128) * 128
    steps = 2 * far - 1
    vm, dma = pltpu.VMEM, pltpu.SemaphoreType.DMA
    scratch = [
        vm((2, n_tok), jnp.int32), vm((2, n_tok), F32),
        vm((hid, slots), BF), vm((hid, slots), BF), vm((hid, slots), BF),
        vm((hid, model), BF), vm((hid, model), BF), vm((hid, model), BF), vm((hid, model), BF), vm((hid, model), BF),
        vm((model, toks), BF),
        vm((model, slots), BF), vm((model // 2, slots), BF), vm((2, model, part), BF), vm((2, model // 2, part), BF),
        vm((2, steps, half, slots), BF), vm((2, steps, half, slots), BF),
        vm((2, 2, steps, half, part), BF), vm((2, 2, steps, half, part), BF),
        vm((hid, slots), BF), vm((hid, slots), BF), vm((wide, slots), BF),
        vm((slots, wide), BF), vm((slots, wide), BF), vm((slots, wide), BF), vm((slots, wide), BF),
        vm((slots, n_tok), BF), vm((slots, n_tok), BF), vm((slots, slots), BF),
        pltpu.SemaphoreType.REGULAR((3,)), dma((11,)),
        dma((2, 2, far, 2)), dma((2, 2, far, 2)), dma((2, 1 + 4 * far)), dma((2, 1 + 4 * far)),
        dma((nx,)), dma((nx,)), dma((2, nx)), dma((2, nx)),
        dma((2, steps)), dma((2, steps)), dma((2, 2, steps)), dma((2, 2, steps)),
        dma((ny,)), dma((ny,)), dma((nz,)), dma((nz,)),
    ]
    return pl.pallas_call(
        functools.partial(kernel, nx, ny, nz, cap),
        out_shape=(pltpu.VMEM((feat, n_tok), BF), pltpu.VMEM((feat, toks), BF)),
        in_specs=[pl.BlockSpec(memory_space=pltpu.HBM)] * 11,
        out_specs=(pl.BlockSpec(memory_space=pltpu.VMEM), pl.BlockSpec(memory_space=pltpu.VMEM)),
        scratch_shapes=scratch,
        compiler_params=pltpu.CompilerParams(
            collective_id=0, has_side_effects=True, vmem_limit_bytes=62 * 1024 * 1024
        ),
    )(routes.T, gate_scores.T, back_hidden, saved_gate, saved_up, egw, euw, inputs_b, dgw, duw, ddw)


def solution(mesh):
    both = ("expert", "tensor")
    in_specs = (
        P(both, None), P(both, None),
        P(both, "dp", None), P(both, "dp", None), P(both, "dp", None), P(both, "dp", None), P(both, "dp", None),
        P("dp", both), P("dp", None), P("dp", None), P("dp", None),
    )
    out_specs = (P("dp", both), P("dp", both))
    body = functools.partial(local, mesh.shape["expert"], mesh.shape["tensor"])
    return jax.shard_map(body, mesh=mesh, in_specs=in_specs, out_specs=out_specs, check_vma=False)
```
